128 devices in a mesh: dp: 4 (over y), slab: 32 (over x, z, core).
Axes of the slice: x: 4, y: 4, z: 4, core: 2. Of those that a mesh axis runs over, the one named last changes fastest.
Arguments:
- volume: bfloat16 [4, 64, 16, 32, 256], P('dp', 'slab'), may hold values from -6 to 6
- pre_act: bfloat16 [4, 64, 16, 32, 256], P('dp', 'slab'), may hold values from -6 to 6
- cotangent: bfloat16 [4, 64, 16, 32, 256], P('dp', 'slab'), may hold values from -0.29882812 to 0.29882812
- kernel_second: bfloat16 [27, 256, 256], replicated, may hold values from -0.078125 to 0.078125
- q_start: float32 [2, 256, 32], replicated, may hold values from -6 to 6
- error: bfloat16 [4, 32, 2, 6912, 256], P('dp', 'slab'), may hold values from -3 to 3
Outputs:
- summed_gradient: float32 [2, 6912, 256], P(None, 'slab')
- new_error: bfloat16 [4, 32, 2, 6912, 256], P('dp', 'slab')
The draws below stay inside these ranges and needn't reach their ends.
All inputs are finite; a program needn't handle non-finite values.
Results may differ from the reference program's by a relative error of at most 0.0036.
Values may be sent and summed in bfloat16 or wider, within the bound.
A program may use at most 128 MiB of HBM per device.

```python
import jax
import jax.numpy as jnp
from jax import lax

C = 256
RANK = 32
DD = 2
HH = 16
WW = 32
ROWS = 6912
DEPTH = 64
N_DP = 4
N_SLAB = 32


def level_of(key, extent, cuts, smallest, top_value):
    gain, own = 1.0, jax.random.fold_in(key, 6)
    for axis_at, blocks in cuts:
        steps = jnp.exp(jax.random.uniform(jax.random.fold_in(own, axis_at), (blocks,), jnp.float32, smallest / len(cuts), top_value / len(cuts)))
        gain = gain * jnp.repeat(steps, extent[axis_at] // blocks).reshape([-1 if axis == axis_at else 1 for axis in range(len(extent))])
    return gain


def gaussian(stream_key, extent, width, bound, shards=(), dtype=jnp.bfloat16):
    result = jax.random.normal(stream_key, extent, jnp.float32) * width
    if len(shards) > 0:
        result = level_of(stream_key, extent, shards, -0.22, 0.18) * result
    return jnp.clip(result, min=-bound, max=bound).astype(dtype)


def setup_inputs(seed: int = 0) -> dict:
    key_of = jax.random.split(jax.random.key(seed), 7)
    volume = gaussian(key_of[0], (N_DP, DEPTH, HH, WW, C), 1.0, 6.0, ((0, 4), (1, 32)))
    pre_act = gaussian(key_of[1], (N_DP, DEPTH, HH, WW, C), 1.0, 6.0, ((0, 4), (1, 32)))
    cotangent = gaussian(key_of[2], (N_DP, DEPTH, HH, WW, C), 0.05, 0.29882812, ((0, 4), (1, 32)))
    kernel_second = gaussian(key_of[3], (27, C, C), (27 * C) ** -0.5, 0.078125)
    q_start = gaussian(key_of[4], (2, C, RANK), 1.0, 6.0, (), jnp.float32)
    error = gaussian(key_of[5], (N_DP, N_SLAB, 2, ROWS, C), 0.5, 3.0, ((0, 4), (1, 32)))
    return dict(volume=volume, pre_act=pre_act, cotangent=cotangent, kernel_second=kernel_second, q_start=q_start, error=error)


def tap_slice(padded, start_a, start_b, start_c):
    return padded[start_a:start_a + DEPTH, start_b:start_b + HH, start_c:start_c + WW]

def pad_cells(field):
    return jnp.pad(field, ((1, 1), (1, 1), (1, 1), (0, 0)))

def slab_grads(source, out_rows):
    padded = pad_cells(source)
    terms = []
    for k in range(27):
        piece = tap_slice(padded, k // 9, k // 3 % 3, k % 3)
        piece = piece.astype(jnp.float32).reshape(N_SLAB, DD * HH * WW, C)
        terms.append(jnp.einsum('snc,snd->scd', piece, out_rows))
    return jnp.stack(terms, axis=1).reshape(N_SLAB, 27 * C, C)

def volume_grads(volume, pre_act, cotangent, kernel_second):
    act = jnp.maximum(pre_act, jnp.zeros_like(pre_act))
    cot_rows = cotangent.astype(jnp.float32).reshape(N_SLAB, DD * HH * WW, C)
    grad_second = slab_grads(act, cot_rows)
    cot_pad = pad_cells(cotangent)
    back = jnp.zeros((DEPTH * HH * WW, C), jnp.float32)
    for k in range(27):
        piece = tap_slice(cot_pad, 2 - k // 9, 2 - k // 3 % 3, 2 - k % 3).reshape(DEPTH * HH * WW, C)
        back = back + jnp.dot(piece.astype(jnp.float32), kernel_second[k].T.astype(jnp.float32), preferred_element_type=jnp.float32)
    back = back.reshape(DEPTH, HH, WW, C)
    gate = jnp.where(pre_act > 0, back, jnp.zeros_like(back)).astype(jnp.bfloat16)
    gate_rows = gate.astype(jnp.float32).reshape(N_SLAB, DD * HH * WW, C)
    grad_first = slab_grads(volume, gate_rows)
    return jnp.stack([grad_first, grad_second], axis=1)

def orthonormal(p_sum):
    highest = lax.Precision.HIGHEST
    gram = jnp.einsum('rq,rs->qs', p_sum, p_sum, precision=highest)
    lower = jnp.linalg.cholesky(gram)
    return lax.linalg.triangular_solve(lower, p_sum, left_side=False, lower=True, transpose_a=True)

def reference(volume, pre_act, cotangent, kernel_second, q_start, error):
    highest = lax.Precision.HIGHEST
    grads = jnp.stack([volume_grads(volume[d], pre_act[d], cotangent[d], kernel_second) for d in range(N_DP)])
    matrix = grads + error.astype(jnp.float32)
    p_sum = jnp.einsum('abLrc,Lcq->abLrq', matrix, q_start, precision=highest).sum(axis=(0, 1))
    p_hat = jnp.stack([orthonormal(p_sum[0]), orthonormal(p_sum[1])])
    q_sum = jnp.einsum('abLrc,Lrq->abLcq', matrix, p_hat, precision=highest).sum(axis=(0, 1))
    summed = jnp.einsum('Lrq,Lcq->Lrc', p_hat, q_sum, precision=highest)
    new_error = (matrix - summed / (N_DP * N_SLAB)).astype(jnp.bfloat16)
    return (summed, new_error)
```

```python
import functools

import jax
import jax.numpy as jnp
from jax import lax
from jax.experimental import pallas as pl
from jax.experimental.pallas import tpu as pltpu
from jax.sharding import PartitionSpec as P

BF, F32 = jnp.bfloat16, jnp.float32
MESH = pl.DeviceIdType.MESH
NT = (((1,), (1,)), ((), ()))
TN = (((0,), (0,)), ((), ()))
NN = (((1,), (0,)), ((), ()))
C, RANK, CELLS, WW, ROWS = 256, 32, 512, 32, 6912
PAD = CELLS + 2 * WW
HALF = ROWS // 2
QUART = 896


def mm(x, y, dims=NN):
    return lax.dot_general(x, y, dims, preferred_element_type=F32)


def split(x):
    hi = x.astype(BF)
    return hi, (x - hi.astype(F32)).astype(BF)


def precise(x, y, dims=NN):
    xh, xl = split(x)
    yh, yl = split(y)
    return mm(xh, yh, dims) + (mm(xh, yl, dims) + mm(xl, yh, dims))


def store_shifts(dst, plane, x):
    w = lax.broadcasted_iota(jnp.int32, (CELLS, C), 0) % WW
    wide = x.astype(F32)
    up = jnp.where(w == WW - 1, 0.0, pltpu.roll(wide, CELLS - 1, 0))
    down = jnp.where(w == 0, 0.0, pltpu.roll(wide, 1, 0))
    zero = jnp.zeros((WW, C), BF)
    for c, piece in enumerate((up.astype(BF), x, down.astype(BF))):
        dst[c, plane, 0:WW, :] = zero
        dst[c, plane, WW : WW + CELLS, :] = piece
        dst[c, plane, WW + CELLS : PAD, :] = zero


class Places:
    def __init__(self):
        self.y = lax.axis_index("dp")
        self.s = lax.axis_index("slab")
        self.x = self.s // 8
        self.z = (self.s // 2) % 4
        self.core = self.s % 2

    def at(self, dy, dx, dz, dcore=0):
        y = (self.y + dy) % 4
        x = (self.x + dx) % 4
        z = (self.z + dz) % 4
        core = (self.core + dcore) % 2
        return {"dp": y, "slab": x * 8 + z * 2 + core}

    def slab(self, step):
        return {"dp": self.y, "slab": (self.s + step + 32) % 32}


def main_kernel(
    pre_hbm, cot_hbm, vol_hbm, ker_hbm, err_hbm, qt_ref,
    mat_hbm, left_hbm, right_out,
    act, cot, vol, ker, err, cv, gv, bq, mat, send, r0, r1, a1, r2, r3, g2, fin, flat,
    srcv, sall, inv, local_sem, halo_send, halo_recv, ar_send, ar_recv, s_send, s_recv,
):
    me = Places()
    s, core = me.s, me.core

    loads = []
    for i, (src, dst) in enumerate(
        (
            (cot_hbm, cot.at[1:3]),
            (err_hbm.at[1], err.at[1]),
            (pre_hbm, act.at[1:3]),
            (err_hbm.at[0], err.at[0]),
            (ker_hbm, ker),
            (vol_hbm, vol.at[1:3]),
        )
    ):
        copy = pltpu.make_async_copy(src, dst, local_sem.at[i])
        copy.start()
        loads.append(copy)

    barrier = pltpu.get_barrier_semaphore()
    peers = [me.slab(-1), me.slab(1), me.at(0, 0, 0, 1)]
    for i in range(1, 4):
        peers += [me.at(i, 0, 0), me.at(0, i, 0), me.at(0, 0, i)]
    for peer in peers:
        pl.semaphore_signal(barrier, inc=1, device_id=peer, device_id_type=MESH)
    pl.semaphore_wait(barrier, len(peers))

    halos = []
    for i, (src, dst) in enumerate(((cot_hbm, cot), (pre_hbm, act), (vol_hbm, vol))):
        pair = []
        for j, (plane, slot, step) in enumerate(((1, 0, 1), (0, 3, -1))):
            copy = pltpu.make_async_remote_copy(
                src_ref=src.at[plane], dst_ref=dst.at[slot],
                send_sem=halo_send.at[i, j], recv_sem=halo_recv.at[i, j],
                device_id=me.slab(step), device_id_type=MESH,
            )
            copy.start()
            pair.append(copy)
        halos.append(pair)

    def wait_halo(i):
        for copy in halos[i]:
            copy.wait()

    def masked(ref, plane):
        if plane == 0:
            return jnp.where(s > 0, ref[0], jnp.zeros((CELLS, C), BF))
        if plane == 3:
            return jnp.where(s < 31, ref[3], jnp.zeros((CELLS, C), BF))
        return ref[plane]

    q2 = [jnp.concatenate(split(qt_ref[l]), 0) for l in range(2)]

    def lanes_of(k):
        if k < 13:
            return ((0, k * 256, 0, 256),)
        if k == 13:
            return ((0, k * 256, 0, 128), (1, 0, 128, 256))
        return ((1, k * 256 - HALF, 0, 256),)

    def put_left(l, k, value, add):
        for g in range(4):
            for lh, lane, lo, hi in lanes_of(k):
                where = (l, g // 2, g % 2 * 2 + lh, slice(None), slice(lane, lane + hi - lo))
                piece = value[8 * g : 8 * g + 8, lo:hi]
                send[where] = send[where] + piece if add else piece

    def error_left(l):
        for k in range(27):
            t = mm(q2[l], err[l, k * 256 : (k + 1) * 256, :], NT)
            put_left(l, k, t[:RANK] + t[RANK:], False)

    def right_factor(l, source, first):
        for d in range(2):
            parts = []
            for c in range(3):
                t = mm(source[c, first + d, WW : WW + CELLS, :], q2[l], NT)
                parts += list(split(t[:, :RANK] + t[:, RANK:]))
            bq[l, d, 0:WW, :] = jnp.zeros((WW, 6 * RANK), BF)
            bq[l, d, WW : WW + CELLS, :] = jnp.concatenate(parts, 1)
            bq[l, d, WW + CELLS : PAD, :] = jnp.zeros((WW, 6 * RANK), BF)

    def grad_left(l, planes):
        for a in range(3):
            for b in range(3):
                r = (2 - b) * WW
                x = bq[l, :, r : r + CELLS, :].reshape(2 * CELLS, 6 * RANK)
                t = mm(x, planes[a : a + 2].reshape(2 * CELLS, C), TN)
                for c in range(3):
                    piece = t[64 * c : 64 * c + 32] + t[64 * c + 32 : 64 * c + 64]
                    put_left(l, 9 * a + 3 * b + c, piece, True)

    one = 1 - core
    i1 = me.y * one + me.x * core
    i2 = me.x * one + me.z * core
    i3 = me.z * one + me.y * core

    def axis_peer(axis, i):
        if axis == 1:
            return me.at(i * one, i * core, 0)
        if axis == 2:
            return me.at(0, i * one, i * core)
        return me.at(i * core, 0, i * one)

    pending = []

    def push(src, dst, sems, l, n, peer):
        copy = pltpu.make_async_remote_copy(
            src_ref=src, dst_ref=dst, send_sem=sems[0].at[l, n], recv_sem=sems[1].at[l, n],
            device_id=peer, device_id_type=MESH,
        )
        copy.start()
        pending.append(copy)
        return copy

    ar_sems = (ar_send, ar_recv)

    def all_reduce(l):
        copy = push(send.at[l, one], r0.at[l], ar_sems, l, 0, me.at(0, 0, 0, 1))
        yield
        copy.wait_recv()
        for j in range(4):
            send[l, core, j] = send[l, core, j] + r0[l, j]
        copies = [
            push(send.at[l, core, (i1 + i) % 4], r1.at[l, i - 1], ar_sems, l, i, axis_peer(1, i))
            for i in range(1, 4)
        ]
        yield
        for copy in copies:
            copy.wait_recv()
        total = send[l, core, i1] + r1[l, 0] + r1[l, 1] + r1[l, 2]
        for j in range(3):
            a1[l, j] = total[:, QUART * j : QUART * (j + 1)]
        a1[l, 3] = jnp.concatenate([total[:, QUART * 3 :], jnp.zeros((8, 128), F32)], 1)
        copies = [
            push(a1.at[l, (i2 + i) % 4], r2.at[l, i - 1], ar_sems, l, 3 + i, axis_peer(2, i))
            for i in range(1, 4)
        ]
        yield
        for copy in copies:
            copy.wait_recv()
        r3[l, i3] = a1[l, i2] + r2[l, 0] + r2[l, 1] + r2[l, 2]
        copies = [
            push(r3.at[l, i3], r3.at[l, i3], ar_sems, l, 6 + i, axis_peer(3, i))
            for i in range(1, 4)
        ]
        yield
        for copy in copies:
            copy.wait_recv()
        g2[l, i2] = r3[l, 0] + r3[l, 1] + r3[l, 2] + r3[l, 3]
        copies = [
            push(g2.at[l, i2], g2.at[l, i2], ar_sems, l, 9 + i, axis_peer(2, i))
            for i in range(1, 4)
        ]
        yield
        for copy in copies:
            copy.wait_recv()
        for j in range(3):
            fin[l, core, i1, :, QUART * j : QUART * (j + 1)] = g2[l, j]
        fin[l, core, i1, :, QUART * 3 : HALF] = g2[l, 3, :, : HALF - 3 * QUART]
        copies = [
            push(
                fin.at[l, core, i1], fin.at[l, core, i1], ar_sems, l, 12 + i, axis_peer(1, i)
            )
            for i in range(1, 4)
        ]
        yield
        for copy in copies:
            copy.wait_recv()
        copy = push(fin.at[l, core], fin.at[l, core], ar_sems, l, 16, me.at(0, 0, 0, 1))
        yield
        copy.wait_recv()
        for h in range(2):
            for lh in range(2):
                hi, lo = split(jnp.concatenate([fin[l, h, lh], fin[l, h, 2 + lh]], 0))
                lanes = slice(HALF * lh, HALF * (lh + 1))
                flat[l, 16 * h : 16 * h + 16, lanes] = hi
                flat[l, RANK + 16 * h : RANK + 16 * h + 16, lanes] = lo
        yield

    def grad_step(l, planes, source, first, i):
        b, c = i // 3, i % 3
        r = (2 - b) * WW
        right = source[c, first : first + 2, r : r + CELLS, :].reshape(2 * CELLS, C)
        for a in range(3):
            rows = slice((9 * a + i) * 256, (9 * a + i + 1) * 256)
            g = mm(planes[a : a + 2].reshape(2 * CELLS, C), right, TN)
            mat[l, rows, :] = g + err[l, rows, :].astype(F32)

    loads[0].wait()
    for plane in (1, 2):
        store_shifts(cv, plane, cot[plane])
    loads[1].wait()
    error_left(1)
    right_factor(1, cv, 1)
    loads[3].wait()
    error_left(0)
    wait_halo(0)
    for plane in (0, 3):
        store_shifts(cv, plane, masked(cot, plane))
    loads[2].wait()
    wait_halo(1)
    for plane in range(4):
        act[plane] = jnp.maximum(masked(act, plane), jnp.zeros((CELLS, C), BF))
    grad_left(1, act)
    second = all_reduce(1)
    next(second)

    loads[4].wait()
    for d in range(2):
        total = None
        for a in range(3):
            x = jnp.concatenate(
                [
                    cv[c, d + 2 - a, (2 - b) * WW : (2 - b) * WW + CELLS, :]
                    for b in range(3)
                    for c in range(3)
                ],
                1,
            )
            w = jnp.concatenate([ker[9 * a + i] for i in range(9)], 1)
            t = mm(x, w, NT)
            total = t if total is None else total + t
        gate = jnp.where(act[1 + d] > 0, total, 0.0).astype(BF)
        store_shifts(gv, d, gate)
        next(second)
    right_factor(0, gv, 0)
    loads[5].wait()
    wait_halo(2)
    for plane in (0, 3):
        vol[plane] = masked(vol, plane)
    next(second)
    grad_left(0, vol)
    next(second)
    first = all_reduce(0)
    next(first)

    for i in range(9):
        grad_step(1, act, cv, 1, i)
        if i in (2, 5, 8):
            next(second)
            next(first)
    stores = [pltpu.make_async_copy(mat.at[1], mat_hbm.at[1], local_sem.at[6])]
    stores[0].start()
    for i in range(9):
        grad_step(0, vol, gv, 0, i)
        if i in (2, 5, 8):
            next(first)
    stores.append(pltpu.make_async_copy(mat.at[0], mat_hbm.at[0], local_sem.at[7]))
    stores[1].start()

    def right_terms(l):
        acc = jnp.zeros((RANK, C), F32)
        gram = jnp.zeros((2 * RANK, 2 * RANK), F32)
        for k in range(27):
            mh, ml = split(mat[l, k * 256 : (k + 1) * 256, :])
            both = flat[l, :, k * 256 : (k + 1) * 256]
            t = mm(both, mh)
            acc = acc + (t[:RANK] + (t[RANK:] + mm(both[:RANK], ml)))
            gram = gram + mm(both, both, NT)
        srcv[l] = acc
        return (gram[:RANK, :RANK] + gram[RANK:, RANK:]) + (
            gram[:RANK, RANK:] + gram[RANK:, :RANK]
        )

    gram_second = right_terms(1)
    next(first)
    gram_first = right_terms(0)
    left_copy = pltpu.make_async_copy(flat, left_hbm, local_sem.at[8])
    left_copy.start()

    s_sems = (s_send, s_recv)
    copy = push(srcv.at[one], sall.at[0, 0], s_sems, 0, 0, me.at(0, 0, 0, 1))
    eye = (
        lax.broadcasted_iota(jnp.int32, (RANK, RANK), 0)
        == lax.broadcasted_iota(jnp.int32, (RANK, RANK), 1)
    ).astype(F32)
    tables = [jnp.concatenate([g, eye], 1) for g in (gram_first, gram_second)]
    rows = lax.broadcasted_iota(jnp.int32, (RANK, 2 * RANK), 0)

    def eliminate(j0, j1):
        for j in range(j0, j1):
            for l in range(2):
                t = tables[l]
                row = t[j : j + 1, :] * (1.0 / t[j : j + 1, j : j + 1])
                tables[l] = jnp.where(rows == j, row, t - t[:, j : j + 1] * row)

    eliminate(0, 8)
    copy.wait_recv()
    mine = srcv[core] + sall[0, 0]
    for n, (index, step) in enumerate(((me.y, (1, 0, 0)), (me.x, (0, 1, 0)), (me.z, (0, 0, 1)))):
        sall[1 + n, index] = mine
        copies = [
            push(
                sall.at[1 + n, index], sall.at[1 + n, index], s_sems, 1 + n, i,
                me.at(*(i * v for v in step)),
            )
            for i in range(1, 4)
        ]
        eliminate(8 + 8 * n, 16 + 8 * n)
        for copy in copies:
            copy.wait_recv()
        mine = (sall[1 + n, 0] + sall[1 + n, 1]) + (sall[1 + n, 2] + sall[1 + n, 3])
    inv[core] = mine
    copy = push(inv.at[core], inv.at[core], s_sems, 4, 0, me.at(0, 0, 0, 1))
    copy.wait_recv()
    for l in range(2):
        right_out[l] = precise(tables[l][:, RANK:], inv[l])

    for copy in pending:
        copy.wait_send()
    for copy in stores:
        copy.wait()
    left_copy.wait()


def last_kernel(start_ref, mat_ref, left_ref, right_ref, err_out, sum_out, span):
    l, i = pl.program_id(0), pl.program_id(1)
    wh, wl = split(right_ref[l])
    right = jnp.concatenate([wl, wh, wh], 0)

    def product(lane, width):
        both = left_ref[l, :, pl.ds(lane, width)]
        return mm(jnp.concatenate([both[:RANK], both], 0), right, TN)

    width = mat_ref.shape[1]
    lane = pl.multiple_of(i * width, 256)
    err_out[0] = (mat_ref[0] - product(lane, width) * (1.0 / 128)).astype(BF)

    @pl.when(i == 0)
    def _():
        start = start_ref[0]
        base = jnp.minimum(start // 256, 25) * 256
        span[...] = product(pl.multiple_of(base, 256), 512)
        sum_out[l] = span[pl.ds(pl.multiple_of(start - base, 8), 216), :]


def per_device(volume, pre_act, cotangent, kernel_second, q_start, error):
    def rows(x):
        return x.reshape(2, CELLS, C)

    any_spec = pl.BlockSpec(memory_space=pl.ANY)
    vmem = pl.BlockSpec(memory_space=pltpu.VMEM)
    dma = pltpu.SemaphoreType.DMA
    V = pltpu.VMEM
    mat, left, right = pl.pallas_call(
        main_kernel,
        out_shape=(
            jax.ShapeDtypeStruct((2, ROWS, C), F32),
            jax.ShapeDtypeStruct((2, 2 * RANK, ROWS), BF),
            jax.ShapeDtypeStruct((2, RANK, C), F32),
        ),
        in_specs=[any_spec] * 5 + [vmem],
        out_specs=(any_spec, any_spec, vmem),
        scratch_shapes=[
            V((4, CELLS, C), BF), V((4, CELLS, C), BF), V((4, CELLS, C), BF),
            V((27, C, C), BF), V((2, ROWS, C), BF),
            V((3, 4, PAD, C), BF), V((3, 2, PAD, C), BF), V((2, 2, PAD, 6 * RANK), BF),
            V((2, ROWS, C), F32),
            V((2, 2, 4, 8, HALF), F32), V((2, 4, 8, HALF), F32), V((2, 3, 8, HALF), F32),
            V((2, 4, 8, QUART), F32), V((2, 3, 8, QUART), F32), V((2, 4, 8, QUART), F32),
            V((2, 4, 8, QUART), F32), V((2, 2, 4, 8, HALF), F32), V((2, 2 * RANK, ROWS), BF),
            V((2, RANK, C), F32), V((4, 4, RANK, C), F32), V((2, RANK, C), F32),
            dma((9,)), dma((3, 2)), dma((3, 2)), dma((2, 17)), dma((2, 17)),
            dma((5, 4)), dma((5, 4)),
        ],
        compiler_params=pltpu.CompilerParams(
            collective_id=0, has_side_effects=True, vmem_limit_bytes=60 << 20
        ),
        name="main_kernel",
    )(
        rows(pre_act), rows(cotangent), rows(volume), kernel_second,
        error.reshape(2, ROWS, C), jnp.swapaxes(q_start, 1, 2),
    )
    start = (lax.axis_index("slab") * (ROWS // 32)).astype(jnp.int32).reshape(1)
    width = 768
    new_error, summed = pl.pallas_call(
        last_kernel,
        grid=(2, ROWS // width),
        out_shape=(
            jax.ShapeDtypeStruct((2, ROWS, C), BF),
            jax.ShapeDtypeStruct((2, ROWS // 32, C), F32),
        ),
        in_specs=[
            pl.BlockSpec(memory_space=pltpu.SMEM),
            pl.BlockSpec((1, width, C), lambda l, i: (l, i, 0)),
            vmem,
            vmem,
        ],
        out_specs=(
            pl.BlockSpec((1, width, C), lambda l, i: (l, i, 0)),
            pl.BlockSpec((2, ROWS // 32, C), lambda l, i: (0, 0, 0)),
        ),
        scratch_shapes=[V((512, C), F32)],
        compiler_params=pltpu.CompilerParams(vmem_limit_bytes=32 << 20),
        name="last_kernel",
    )(start, mat, left, right)
    return (summed, new_error.reshape(1, 1, 2, ROWS, C))


def solution(mesh):
    in_specs = (
        P("dp", "slab", None, None, None),
        P("dp", "slab", None, None, None),
        P("dp", "slab", None, None, None),
        P(),
        P(),
        P("dp", "slab", None, None, None),
    )
    out_specs = (P(None, "slab", None), P("dp", "slab", None, None, None))
    return jax.shard_map(
        per_device, mesh=mesh, in_specs=in_specs, out_specs=out_specs, check_vma=False
    )
```

```python
import functools

import jax
import jax.numpy as jnp
from jax import lax
from jax.experimental import pallas as pl
from jax.experimental.pallas import tpu as pltpu
from jax.sharding import PartitionSpec as P

BF, F32 = jnp.bfloat16, jnp.float32
MESH = pl.DeviceIdType.MESH
NT = (((1,), (1,)), ((), ()))
TN = (((0,), (0,)), ((), ()))
NN = (((1,), (0,)), ((), ()))
C, RANK, CELLS, WW, ROWS = 256, 32, 512, 32, 6912
PAD = CELLS + 2 * WW
STEP = 9
MAIN_VMEM, LAST_VMEM = 42, 24


def mm(x, y, dims=NN):
    return lax.dot_general(x, y, dims, preferred_element_type=F32)


def split(x):
    hi = x.astype(BF)
    return hi, (x - hi.astype(F32)).astype(BF)


def precise(x, y, dims=NN):
    xh, xl = split(x)
    yh, yl = split(y)
    return mm(xh, yh, dims) + (mm(xh, yl, dims) + mm(xl, yh, dims))


def store_shifts(dst, plane, x):
    w = lax.broadcasted_iota(jnp.int32, (CELLS, C), 0) % WW
    wide = x.astype(F32)
    up = jnp.where(w == WW - 1, 0.0, pltpu.roll(wide, CELLS - 1, 0))
    down = jnp.where(w == 0, 0.0, pltpu.roll(wide, 1, 0))
    zero = jnp.zeros((WW, C), BF)
    for c, piece in enumerate((up.astype(BF), x, down.astype(BF))):
        dst[c, plane, 0:WW, :] = zero
        dst[c, plane, WW : WW + CELLS, :] = piece
        dst[c, plane, WW + CELLS : PAD, :] = zero


class Places:
    def __init__(self):
        self.y = lax.axis_index("dp")
        self.s = lax.axis_index("slab")
        self.x = self.s // 8
        self.z = (self.s // 2) % 4
        self.core = self.s % 2

    def at(self, dy, dx, dz, dcore=0):
        y = (self.y + dy) % 4
        x = (self.x + dx) % 4
        z = (self.z + dz) % 4
        core = (self.core + dcore) % 2
        return {"dp": y, "slab": x * 8 + z * 2 + core}

    def slab(self, step):
        return {"dp": self.y, "slab": (self.s + step + 32) % 32}


def main_kernel(
    pre_hbm, cot_hbm, vol_hbm, ker_hbm, err_hbm, qt_ref,
    mat, flat, right_out,
    act, cot, vol, ker, err, cv, gv, bq, acc, send, r0, r1, r2, fin,
    srcv, sall, inv, local_sem, halo_send, halo_recv, pair_send, pair_recv, ar_send, ar_recv,
    s_send, s_recv,
):
    me = Places()
    s, core = me.s, me.core
    one = 1 - core

    loads = []
    for i, (src, dst) in enumerate(
        (
            (cot_hbm, cot.at[1:3]),
            (ker_hbm, ker),
            (err_hbm.at[0], err.at[0]),
            (vol_hbm, vol.at[1:3]),
            (pre_hbm, act.at[1:3]),
            (err_hbm.at[1], err.at[1]),
        )
    ):
        copy = pltpu.make_async_copy(src, dst, local_sem.at[i])
        copy.start()
        loads.append(copy)

    barrier = pltpu.get_barrier_semaphore()
    peers = [me.slab(-1), me.slab(1), me.at(0, 0, 0, 1)]
    for i in range(1, 4):
        peers += [me.at(i, 0, 0), me.at(0, i, 0), me.at(0, 0, i)]
        peers += [me.at(i * one, j, i * core) for j in range(1, 4)]
    for peer in peers:
        pl.semaphore_signal(barrier, inc=1, device_id=peer, device_id_type=MESH)
    pl.semaphore_wait(barrier, len(peers))

    halos = []
    for i, (src, dst) in enumerate(((cot_hbm, cot), (vol_hbm, vol), (pre_hbm, act))):
        pair = []
        for j, (plane, slot, step) in enumerate(((1, 0, 1), (0, 3, -1))):
            copy = pltpu.make_async_remote_copy(
                src_ref=src.at[plane], dst_ref=dst.at[slot],
                send_sem=halo_send.at[i, j], recv_sem=halo_recv.at[i, j],
                device_id=me.slab(step), device_id_type=MESH,
            )
            copy.start()
            pair.append(copy)
        halos.append(pair)

    def wait_halo(i):
        for copy in halos[i]:
            copy.wait()

    def masked(ref, plane):
        if plane == 0:
            return jnp.where(s > 0, ref[0], jnp.zeros((CELLS, C), BF))
        if plane == 3:
            return jnp.where(s < 31, ref[3], jnp.zeros((CELLS, C), BF))
        return ref[plane]

    q2 = [jnp.concatenate(split(qt_ref[l]), 0) for l in range(2)]

    def error_left(l):
        for k in range(27):
            t = mm(q2[l], err[l, k * 256 : (k + 1) * 256, :], NT)
            send[l, k % 2, k // 2] = t[:RANK] + t[RANK:]
        for k in range(27, 32):
            send[l, k % 2, k // 2] = jnp.zeros((RANK, C), F32)

    def right_factor(l, source, first):
        for d in range(2):
            parts = []
            for c in range(3):
                t = mm(source[c, first + d, WW : WW + CELLS, :], q2[l], NT)
                parts += list(split(t[:, :RANK] + t[:, RANK:]))
            bq[l, d, 0:WW, :] = jnp.zeros((WW, 6 * RANK), BF)
            bq[l, d, WW : WW + CELLS, :] = jnp.concatenate(parts, 1)
            bq[l, d, WW + CELLS : PAD, :] = jnp.zeros((WW, 6 * RANK), BF)

    def grad_left(l, planes, a):
        for b in range(3):
            r = (2 - b) * WW
            x = bq[l, :, r : r + CELLS, :].reshape(2 * CELLS, 6 * RANK)
            t = mm(x, planes[a : a + 2].reshape(2 * CELLS, C), TN)
            for c in range(3):
                k = 9 * a + 3 * b + c
                piece = t[64 * c : 64 * c + 32] + t[64 * c + 32 : 64 * c + 64]
                send[l, k % 2, k // 2] = send[l, k % 2, k // 2] + piece

    i1 = me.y * one + me.x * core
    i2 = me.x * one + me.z * core
    i3 = me.z * one + me.y * core
    here = i1 * 4 + i2
    others = [(i, j) for i in range(4) for j in range(4) if i + j > 0]

    def plane_peer(i, j):
        return me.at(i * one, i * core + j * one, j * core)

    pending = []

    def push(src, dst, sems, l, n, peer):
        copy = pltpu.make_async_remote_copy(
            src_ref=src, dst_ref=dst, send_sem=sems[0].at[l, n], recv_sem=sems[1].at[l, n],
            device_id=peer, device_id_type=MESH,
        )
        copy.start()
        pending.append(copy)
        return copy

    ar_sems = (ar_send, ar_recv)
    pair_sems = (pair_send, pair_recv)
    bounds = (0, 4, 9, 14)

    def pair_step(l, n):
        part = pl.ds(bounds[n], bounds[n + 1] - bounds[n])
        return push(
            send.at[l, one, part], r0.at[l, part], pair_sems, l, n, me.at(0, 0, 0, 1)
        )

    def pair_add(l, n, copy):
        copy.wait_recv()
        for t in range(bounds[n], bounds[n + 1]):
            send[l, core, t] = send[l, core, t] + r0[l, t]

    def all_reduce(l):
        copies = [
            push(
                send.at[l, core, (i1 + i) % 4 * 4 + (i2 + j) % 4], r1.at[l, n],
                ar_sems, l, n, plane_peer(i, j),
            )
            for n, (i, j) in enumerate(others)
        ]
        yield
        total = send[l, core, here]
        for n, copy in enumerate(copies):
            copy.wait_recv()
            total = total + r1[l, n]
        r2[l, i3] = total
        copies = [
            push(
                r2.at[l, i3], r2.at[l, i3], ar_sems, l, 14 + i,
                me.at(i * core, 0, i * one),
            )
            for i in range(1, 4)
        ]
        yield
        for copy in copies:
            copy.wait_recv()
        fin[l, core, here] = (r2[l, 0] + r2[l, 1]) + (r2[l, 2] + r2[l, 3])
        copies = [
            push(
                fin.at[l, core, here], fin.at[l, core, here], ar_sems, l, 18 + n,
                plane_peer(i, j),
            )
            for n, (i, j) in enumerate(others)
        ]
        yield
        for copy in copies:
            copy.wait_recv()
        copy = push(
            fin.at[l, core, 0:14], fin.at[l, core, 0:14], pair_sems, l, 3, me.at(0, 0, 0, 1)
        )
        yield
        copy.wait_recv()
        yield

    def grad_step(l, planes, source, first, i):
        b, c = i // 3, i % 3
        r = (2 - b) * WW
        right = source[c, first : first + 2, r : r + CELLS, :].reshape(2 * CELLS, C)
        for a in range(3):
            rows = slice((9 * a + i) * 256, (9 * a + i + 1) * 256)
            g = mm(planes[a : a + 2].reshape(2 * CELLS, C), right, TN)
            mat[l, rows, :] = g + err[l, rows, :].astype(F32)

    def back_part(d, a):
        x = jnp.concatenate(
            [
                cv[c, d + 2 - a, (2 - b) * WW : (2 - b) * WW + CELLS, :]
                for b in range(3)
                for c in range(3)
            ],
            1,
        )
        w = jnp.concatenate([ker[9 * a + i] for i in range(9)], 1)
        return mm(x, w, NT)

    loads[0].wait()
    for plane in (1, 2):
        store_shifts(cv, plane, cot[plane])
    loads[1].wait()
    acc[0] = back_part(0, 0) + back_part(0, 1)
    acc[1] = back_part(1, 1) + back_part(1, 2)
    loads[2].wait()
    error_left(0)
    wait_halo(0)
    for plane in (0, 3):
        store_shifts(cv, plane, masked(cot, plane))
    loads[4].wait()
    for d in range(2):
        total = acc[d] + back_part(d, 2 - 2 * d)
        store_shifts(gv, d, jnp.where(act[1 + d] > 0, total, 0.0).astype(BF))
    right_factor(0, gv, 0)
    loads[3].wait()
    wait_halo(1)
    for plane in (0, 3):
        vol[plane] = masked(vol, plane)
    pairs = []
    for a in range(3):
        grad_left(0, vol, a)
        pairs.append(pair_step(0, a))
        if a > 0:
            pair_add(0, a - 1, pairs[a - 1])
    loads[5].wait()
    error_left(1)
    right_factor(1, cv, 1)
    pair_add(0, 2, pairs[2])
    first = all_reduce(0)
    next(first)
    wait_halo(2)
    for plane in range(4):
        act[plane] = jnp.maximum(masked(act, plane), jnp.zeros((CELLS, C), BF))
    pairs = []
    for a in range(3):
        grad_left(1, act, a)
        pairs.append(pair_step(1, a))
        if a > 0:
            pair_add(1, a - 1, pairs[a - 1])
    grad_step(0, vol, gv, 0, 0)
    grad_step(0, vol, gv, 0, 1)
    pair_add(1, 2, pairs[2])
    second = all_reduce(1)
    next(second)
    for i in range(2, 7):
        grad_step(0, vol, gv, 0, i)
    next(first)
    for i in range(7, 9):
        grad_step(0, vol, gv, 0, i)
    for i in range(0, 2):
        grad_step(1, act, cv, 1, i)
    next(second)
    for i in range(2, 5):
        grad_step(1, act, cv, 1, i)
    next(first)
    for i in range(5, 9):
        grad_step(1, act, cv, 1, i)
    next(second)
    next(first)

    def right_tap(l, k, hand, tap, sums):
        mh, ml = split(mat[l, pl.ds(pl.multiple_of(k * 256, 256), 256), :])
        both = jnp.concatenate(split(fin[l, hand, tap]), 0)
        flat[l, k] = both
        t = mm(both, mh)
        return (
            sums[0] + (t[:RANK] + (t[RANK:] + mm(both[:RANK], ml))),
            sums[1] + mm(both, both, NT),
        )

    def right_half(l, hand, sums):
        for t in range(13):
            sums = right_tap(l, 2 * t + hand, hand, t, sums)
        return sums

    def right_done(l, sums):
        srcv[l], gram = right_tap(l, 26, 0, 13, sums)
        return (gram[:RANK, :RANK] + gram[RANK:, RANK:]) + (
            gram[:RANK, RANK:] + gram[RANK:, :RANK]
        )

    zero = (jnp.zeros((RANK, C), F32), jnp.zeros((2 * RANK, 2 * RANK), F32))
    sums_first = right_half(0, core, zero)
    next(first)
    next(second)
    sums_first = right_half(0, one, sums_first)
    gram_first = right_done(0, sums_first)
    sums_second = right_half(1, core, zero)
    next(second)
    gram_second = right_done(1, right_half(1, one, sums_second))

    s_sems = (s_send, s_recv)
    copy = push(srcv.at[one], sall.at[0, 0], s_sems, 0, 0, me.at(0, 0, 0, 1))
    eye = (
        lax.broadcasted_iota(jnp.int32, (RANK, RANK), 0)
        == lax.broadcasted_iota(jnp.int32, (RANK, RANK), 1)
    ).astype(F32)
    tables = [jnp.concatenate([g, eye], 1) for g in (gram_first, gram_second)]
    rows = lax.broadcasted_iota(jnp.int32, (RANK, 2 * RANK), 0)

    def eliminate(j0, j1):
        for j in range(j0, j1):
            for l in range(2):
                t = tables[l]
                row = t[j : j + 1, :] * (1.0 / t[j : j + 1, j : j + 1])
                tables[l] = jnp.where(rows == j, row, t - t[:, j : j + 1] * row)

    eliminate(0, 8)
    copy.wait_recv()
    mine = srcv[core] + sall[0, 0]
    for n, (index, step) in enumerate(((me.y, (1, 0, 0)), (me.x, (0, 1, 0)), (me.z, (0, 0, 1)))):
        sall[1 + n, index] = mine
        copies = [
            push(
                sall.at[1 + n, index], sall.at[1 + n, index], s_sems, 1 + n, i,
                me.at(*(i * v for v in step)),
            )
            for i in range(1, 4)
        ]
        eliminate(8 + 8 * n, 16 + 8 * n)
        for copy in copies:
            copy.wait_recv()
        mine = (sall[1 + n, 0] + sall[1 + n, 1]) + (sall[1 + n, 2] + sall[1 + n, 3])
    inv[core] = mine
    copy = push(inv.at[core], inv.at[core], s_sems, 4, 0, me.at(0, 0, 0, 1))
    copy.wait_recv()
    for l in range(2):
        right_out[l] = precise(tables[l][:, RANK:], inv[l])

    for copy in pending:
        copy.wait_send()


def last_kernel(start_ref, mat_ref, left_ref, right_ref, err_out, sum_out, span):
    l, i = pl.program_id(0), pl.program_id(1)
    wh, wl = split(right_ref[l])
    right = jnp.concatenate([wl, wh, wh], 0)

    def product(k):
        both = left_ref[l, k]
        return mm(jnp.concatenate([both[:RANK], both], 0), right, TN)

    for j in range(STEP):
        k = i * STEP + j
        rows = pl.ds(pl.multiple_of(k * 256, 256), 256)
        value = mat_ref[l, rows, :] - product(k) * (1.0 / 128)
        err_out[0, j * 256 : (j + 1) * 256, :] = value.astype(BF)

    @pl.when(i == 0)
    def _():
        start = start_ref[0]
        k = jnp.minimum(start // 256, 25)
        span[0:256, :] = product(k)
        span[256:512, :] = product(k + 1)
        sum_out[l] = span[pl.ds(pl.multiple_of(start - k * 256, 8), 216), :]


def per_device(volume, pre_act, cotangent, kernel_second, q_start, error):
    def rows(x):
        return x.reshape(2, CELLS, C)

    hbm = pl.BlockSpec(memory_space=pltpu.HBM)
    vmem = pl.BlockSpec(memory_space=pltpu.VMEM)
    dma = pltpu.SemaphoreType.DMA
    V = pltpu.VMEM
    mat, left, right = pl.pallas_call(
        main_kernel,
        out_shape=(
            V((2, ROWS, C), F32),
            V((2, 27, 2 * RANK, C), BF),
            V((2, RANK, C), F32),
        ),
        in_specs=[hbm] * 5 + [vmem],
        out_specs=(vmem, vmem, vmem),
        scratch_shapes=[
            V((4, CELLS, C), BF), V((4, CELLS, C), BF), V((4, CELLS, C), BF),
            V((27, C, C), BF), V((2, ROWS, C), BF),
            V((3, 4, PAD, C), BF), V((3, 2, PAD, C), BF), V((2, 2, PAD, 6 * RANK), BF),
            V((2, CELLS, C), F32),
            V((2, 2, 16, RANK, C), F32), V((2, 14, RANK, C), F32), V((2, 15, RANK, C), F32),
            V((2, 4, RANK, C), F32), V((2, 2, 16, RANK, C), F32),
            V((2, RANK, C), F32), V((4, 4, RANK, C), F32), V((2, RANK, C), F32),
            dma((6,)), dma((3, 2)), dma((3, 2)), dma((2, 4)), dma((2, 4)), dma((2, 33)),
            dma((2, 33)), dma((5, 4)), dma((5, 4)),
        ],
        compiler_params=pltpu.CompilerParams(
            collective_id=0, has_side_effects=True, vmem_limit_bytes=MAIN_VMEM << 20
        ),
        name="main_kernel",
    )(
        rows(pre_act), rows(cotangent), rows(volume), kernel_second,
        error.reshape(2, ROWS, C), jnp.swapaxes(q_start, 1, 2),
    )
    start = (lax.axis_index("slab") * (ROWS // 32)).astype(jnp.int32).reshape(1)
    width = 256 * STEP
    new_error, summed = pl.pallas_call(
        last_kernel,
        grid=(2, 27 // STEP),
        out_shape=(
            jax.ShapeDtypeStruct((2, ROWS, C), BF),
            jax.ShapeDtypeStruct((2, ROWS // 32, C), F32),
        ),
        in_specs=[pl.BlockSpec(memory_space=pltpu.SMEM), vmem, vmem, vmem],
        out_specs=(
            pl.BlockSpec((1, width, C), lambda l, i: (l, i, 0)),
            pl.BlockSpec((2, ROWS // 32, C), lambda l, i: (0, 0, 0)),
        ),
        scratch_shapes=[V((512, C), F32)],
        compiler_params=pltpu.CompilerParams(vmem_limit_bytes=LAST_VMEM << 20),
        name="last_kernel",
    )(start, mat, left, right)
    return (summed, new_error.reshape(1, 1, 2, ROWS, C))


def solution(mesh):
    in_specs = (
        P("dp", "slab", None, None, None),
        P("dp", "slab", None, None, None),
        P("dp", "slab", None, None, None),
        P(),
        P(),
        P("dp", "slab", None, None, None),
    )
    out_specs = (P(None, "slab", None), P("dp", "slab", None, None, None))
    return jax.shard_map(
        per_device, mesh=mesh, in_specs=in_specs, out_specs=out_specs, check_vma=False
    )
```

```python
import functools

import jax
import jax.numpy as jnp
from jax import lax
from jax.experimental import pallas as pl
from jax.experimental.pallas import tpu as pltpu
from jax.sharding import PartitionSpec as P

BF, F32 = jnp.bfloat16, jnp.float32
MESH = pl.DeviceIdType.MESH
NT = (((1,), (1,)), ((), ()))
TN = (((0,), (0,)), ((), ()))
NN = (((1,), (0,)), ((), ()))
C, RANK, CELLS, WW, ROWS = 256, 32, 512, 32, 6912
PAD = CELLS + 2 * WW
MAIN_VMEM, LAST_VMEM = 46, 16


def mm(x, y, dims=NN):
    return lax.dot_general(x, y, dims, preferred_element_type=F32)


def split(x):
    hi = x.astype(BF)
    return hi, (x - hi.astype(F32)).astype(BF)


def precise(x, y, dims=NN):
    xh, xl = split(x)
    yh, yl = split(y)
    return mm(xh, yh, dims) + (mm(xh, yl, dims) + mm(xl, yh, dims))


def store_shifts(dst, plane, x):
    w = lax.broadcasted_iota(jnp.int32, (CELLS, C), 0) % WW
    wide = x.astype(F32)
    up = jnp.where(w == WW - 1, 0.0, pltpu.roll(wide, CELLS - 1, 0))
    down = jnp.where(w == 0, 0.0, pltpu.roll(wide, 1, 0))
    zero = jnp.zeros((WW, C), BF)
    for c, piece in enumerate((up.astype(BF), x, down.astype(BF))):
        dst[c, plane, 0:WW, :] = zero
        dst[c, plane, WW : WW + CELLS, :] = piece
        dst[c, plane, WW + CELLS : PAD, :] = zero


class Places:
    def __init__(self):
        self.y = lax.axis_index("dp")
        self.s = lax.axis_index("slab")
        self.x = self.s // 8
        self.z = (self.s // 2) % 4
        self.core = self.s % 2

    def at(self, dy, dx, dz, dcore=0):
        y = (self.y + dy) % 4
        x = (self.x + dx) % 4
        z = (self.z + dz) % 4
        core = (self.core + dcore) % 2
        return {"dp": y, "slab": x * 8 + z * 2 + core}

    def slab(self, step):
        return {"dp": self.y, "slab": (self.s + step + 32) % 32}


def left_product(both, right):
    return mm(jnp.concatenate([both[:RANK], both], 0), right, TN) * (1.0 / 128)


def stacked_right(right):
    hi, lo = split(right)
    return jnp.concatenate([lo, hi, hi], 0)


def main_kernel(
    pre_hbm, cot_hbm, vol_hbm, ker_hbm, err_hbm, qt_ref,
    mat_first, flat, right_out, tail,
    act, cot, vol, ker, err, cv, gv, bq_first, bq_second, acc, gate, mat_second, send, r0, r1, r2, fin,
    srcv, sall, local_sem, halo_send, halo_recv, pair_send, pair_recv, ar_send, ar_recv,
    s_send, s_recv,
):
    me = Places()
    s, core = me.s, me.core
    one = 1 - core

    loads = []
    for i, (src, dst) in enumerate(
        (
            (cot_hbm, cot.at[1:3]),
            (pre_hbm, act.at[1:3]),
            (err_hbm.at[1], err.at[1]),
            (ker_hbm, ker),
            (err_hbm.at[0], err.at[0]),
            (vol_hbm, vol.at[1:3]),
        )
    ):
        copy = pltpu.make_async_copy(src, dst, local_sem.at[i])
        copy.start()
        loads.append(copy)

    barrier = pltpu.get_barrier_semaphore()
    peers = [me.slab(-1), me.slab(1)]
    for i in range(1, 4):
        peers += [me.at(i, 0, 0), me.at(0, i, 0)]
        for j in range(1, 4):
            peers += [me.at(i, j, 0), me.at(i * one, i * core, j)]
    peers += [me.at(0, 0, i // 2, i % 2) for i in range(1, 8)]
    for peer in peers:
        pl.semaphore_signal(barrier, inc=1, device_id=peer, device_id_type=MESH)
    halos = []

    def send_halos():
        for i, (src, dst) in enumerate(((cot_hbm, cot), (vol_hbm, vol), (pre_hbm, act))):
            pair = []
            for j, (plane, slot, step) in enumerate(((1, 0, 1), (0, 3, -1))):
                copy = pltpu.make_async_remote_copy(
                    src_ref=src.at[plane], dst_ref=dst.at[slot],
                    send_sem=halo_send.at[i, j], recv_sem=halo_recv.at[i, j],
                    device_id=me.slab(step), device_id_type=MESH,
                )
                copy.start()
                pair.append(copy)
            halos.append(pair)

    def wait_halo(i):
        for copy in halos[i]:
            copy.wait()

    def masked(ref, plane):
        if plane == 0:
            return jnp.where(s > 0, ref[0], jnp.zeros((CELLS, C), BF))
        if plane == 3:
            return jnp.where(s < 31, ref[3], jnp.zeros((CELLS, C), BF))
        return ref[plane]

    q2 = [jnp.concatenate(split(qt_ref[l]), 0) for l in range(2)]

    def error_left(l):
        for k in range(27):
            t = mm(q2[l], err[l, k * 256 : (k + 1) * 256, :], NT)
            send[l, k % 2, k // 2] = t[:RANK] + t[RANK:]
        for k in range(27, 32):
            send[l, k % 2, k // 2] = jnp.zeros((RANK, C), F32)

    def right_factor(l, dst, d, x):
        t = mm(x, q2[l], NT)
        t = t[:, :RANK] + t[:, RANK:]
        w = lax.broadcasted_iota(jnp.int32, (CELLS, RANK), 0) % WW
        up = jnp.where(w == WW - 1, 0.0, pltpu.roll(t, CELLS - 1, 0))
        down = jnp.where(w == 0, 0.0, pltpu.roll(t, 1, 0))
        zero = jnp.zeros((WW, 6 * RANK), BF)
        dst[d, 0:WW, :] = zero
        dst[d, WW : WW + CELLS, :] = jnp.concatenate([*split(up), *split(t), *split(down)], 1)
        dst[d, WW + CELLS : PAD, :] = zero

    def grad_left(l, a, factor, planes):
        size = planes.shape[0] * CELLS
        for b in range(3):
            r = (2 - b) * WW
            x = factor[:, r : r + CELLS, :].reshape(size, 6 * RANK)
            t = mm(x, planes[...].reshape(size, C), TN)
            for c in range(3):
                k = 9 * a + 3 * b + c
                piece = t[64 * c : 64 * c + 32] + t[64 * c + 32 : 64 * c + 64]
                send[l, k % 2, k // 2] = send[l, k % 2, k // 2] + piece

    near = [(min(i, 4 - i) + min(j, 4 - j), i, j) for i in range(4) for j in range(4)]
    others = [(i, j) for d, i, j in sorted(near, reverse=True) if d > 0]

    def plane_index(l, hand, i, j):
        if l == 1:
            return (me.y + i) % 4 * 4 + (me.x + j) % 4
        return (me.y * (1 - hand) + me.x * hand + i) % 4 * 4 + (me.z + j) % 4

    def plane_peer(l, i, j):
        return me.at(i, j, 0) if l == 1 else me.at(i * one, i * core, j)

    def axis_index(l):
        return me.z if l == 1 else me.x * one + me.y * core

    def axis_peer(l, i):
        return me.at(0, 0, i) if l == 1 else me.at(i * core, i * one, 0)

    pending, forwards = [], {}

    def push(src, dst, sems, l, n, peer):
        copy = pltpu.make_async_remote_copy(
            src_ref=src, dst_ref=dst, send_sem=sems[0].at[l, n], recv_sem=sems[1].at[l, n],
            device_id=peer, device_id_type=MESH,
        )
        copy.start()
        pending.append(copy)
        return copy

    ar_sems = (ar_send, ar_recv)
    pair_sems = (pair_send, pair_recv)
    bounds = (((0, 4), (4, 9), (9, 14)), ((0, 5), (5, 9), (9, 14)))

    def pair_step(l, n):
        low, high = bounds[l][n]
        part = pl.ds(low, high - low)
        return push(
            send.at[l, one, part], r0.at[l, part], pair_sems, l, n, me.at(0, 0, 0, 1)
        )

    def pair_add(l, n, copy):
        copy.wait_recv()
        for t in range(*bounds[l][n]):
            send[l, core, t] = send[l, core, t] + r0[l, t]

    def all_reduce(l):
        here = plane_index(l, core, 0, 0)
        copies = [
            push(
                send.at[l, core, plane_index(l, core, i, j)], r1.at[l, n],
                ar_sems, l, n, plane_peer(l, i, j),
            )
            for n, (i, j) in enumerate(others)
        ]
        yield
        total = send[l, core, here]
        for n in range(14, -1, -1):
            copies[n].wait_recv()
            total = total + r1[l, n]
        i3 = axis_index(l)
        r2[l, i3] = total
        copies = [
            push(r2.at[l, i3], r2.at[l, i3], ar_sems, l, 14 + i, axis_peer(l, i))
            for i in range(1, 4)
        ]
        yield
        for copy in copies:
            copy.wait_recv()
        fin[l, core, here] = (r2[l, 0] + r2[l, 1]) + (r2[l, 2] + r2[l, 3])
        copies = [
            push(
                fin.at[l, core, here], fin.at[l, core, here], ar_sems, l, 18 + n,
                plane_peer(l, i, j),
            )
            for n, (i, j) in enumerate(others)
        ]
        forward(l, 0, 0, 0)
        yield copies

    def forward(l, n, i, j):
        slot = fin.at[l, core, plane_index(l, core, i, j)]
        forwards[l, n] = push(slot, slot, ar_sems, l, 33 + n, me.at(0, 0, 0, 1))

    def right_tap(l, hand, i, j, sums):
        mat = mat_first if l == 0 else mat_second
        tap = plane_index(l, hand, i, j)
        k = 2 * tap + hand
        row = pl.multiple_of(jnp.minimum(k, 26) * 256, 256)
        mh, ml = split(mat[pl.ds(row, 256), :])
        both = jnp.concatenate(split(fin[l, hand, tap]), 0)
        flat[l, k] = both
        t = mm(both, mh)
        return sums + (t[:RANK] + (t[RANK:] + mm(both[:RANK], ml)))

    def gram_table(l):
        gram = jnp.zeros((2 * RANK, 2 * RANK), F32)
        for k in range(27):
            gram = gram + mm(flat[l, k], flat[l, k], NT)
        gram = (gram[:RANK, :RANK] + gram[RANK:, RANK:]) + (
            gram[:RANK, RANK:] + gram[RANK:, :RANK]
        )
        return jnp.concatenate([gram, eye], 1)

    def right_terms(l, copies, middle=lambda: None):
        sums = jnp.zeros((RANK, C), F32)
        done = [(0, 0)]
        for low, high in ((7, 15), (0, 7)):
            for n in range(high - 1, low - 1, -1):
                sender = others[n]
                source = (-sender[0]) % 4, (-sender[1]) % 4
                copies[n].wait_recv()
                forward(l, 1 + n, *source)
                done.append(source)
            for i, j in done:
                sums = right_tap(l, core, i, j, sums)
            done = []
        rest = [(0, 0)] + [((-i) % 4, (-j) % 4) for i, j in others]
        for n in [0] + list(range(15, 0, -1)):
            forwards[l, n].wait_recv()
        middle()
        for n in [0] + list(range(15, 0, -1)):
            sums = right_tap(l, one, *rest[n], sums)
        srcv[l] = sums

    def right_reduce(l):
        s_sems = (s_send, s_recv)
        mine = srcv[l]
        for n, (index, step) in enumerate(((me.y, (1, 0, 0)), (me.x, (0, 1, 0)))):
            slot = 4 * n + index
            sall[l, slot] = mine
            copies = [
                push(
                    sall.at[l, slot], sall.at[l, slot], s_sems, l, 3 * n + i - 1,
                    me.at(*(i * v for v in step)),
                )
                for i in range(1, 4)
            ]
            yield
            for copy in copies:
                copy.wait_recv()
            mine = (sall[l, 4 * n] + sall[l, 4 * n + 1]) + (sall[l, 4 * n + 2] + sall[l, 4 * n + 3])
        slot = 8 + 2 * me.z + core
        sall[l, slot] = mine
        copies = [
            push(sall.at[l, slot], sall.at[l, slot], s_sems, l, 5 + i, me.at(0, 0, i // 2, i % 2))
            for i in range(1, 8)
        ]
        yield
        for copy in copies:
            copy.wait_recv()
        total = [sall[l, 8 + 2 * i] + sall[l, 9 + 2 * i] for i in range(4)]
        right_out[l] = precise(tables[l][:, RANK:], (total[0] + total[1]) + (total[2] + total[3]))
        yield

    def grad_step(l, planes, source, first, i):
        b, c = i // 3, i % 3
        r = (2 - b) * WW
        right = source[c, first : first + 2, r : r + CELLS, :].reshape(2 * CELLS, C)
        for a in range(3):
            rows = slice((9 * a + i) * 256, (9 * a + i + 1) * 256)
            g = mm(planes[a : a + 2].reshape(2 * CELLS, C), right, TN)
            mat = mat_first if l == 0 else mat_second
            mat[rows, :] = g + err[l, rows, :].astype(F32)

    def back_part(d, a):
        x = jnp.concatenate(
            [
                cv[c, d + 2 - a, (2 - b) * WW : (2 - b) * WW + CELLS, :]
                for b in range(3)
                for c in range(3)
            ],
            1,
        )
        w = jnp.concatenate([ker[9 * a + i] for i in range(9)], 1)
        return mm(x, w, NT)

    loads[0].wait()
    for plane in (1, 2):
        right_factor(1, bq_second, plane, cot[plane])
    loads[1].wait()
    for plane in (1, 2):
        act[plane] = jnp.maximum(act[plane], jnp.zeros((CELLS, C), BF))
    loads[2].wait()
    error_left(1)
    grad_left(1, 1, bq_second[1:3], act[1:3])
    pl.semaphore_wait(barrier, len(peers))
    send_halos()
    pairs = {1: pair_step(1, 1)}
    grad_left(1, 0, bq_second[2:3], act[1:2])
    grad_left(1, 2, bq_second[1:2], act[2:3])
    for plane in (1, 2):
        store_shifts(cv, plane, cot[plane])
    loads[3].wait()
    acc[0] = back_part(0, 0) + back_part(0, 1)
    acc[1] = back_part(1, 1) + back_part(1, 2)
    pair_add(1, 1, pairs[1])
    loads[4].wait()
    error_left(0)
    wait_halo(0)
    for plane in (0, 3):
        right_factor(1, bq_second, plane, masked(cot, plane))
    grad_left(1, 0, bq_second[3:4], act[2:3])
    pairs[0] = pair_step(1, 0)
    grad_left(1, 2, bq_second[0:1], act[1:2])
    pairs[2] = pair_step(1, 2)
    for plane in (0, 3):
        store_shifts(cv, plane, masked(cot, plane))
    total = acc[0] + back_part(0, 2)
    gate[0] = jnp.where(act[1] > 0, total, 0.0).astype(BF)
    pair_add(1, 0, pairs[0])
    pair_add(1, 2, pairs[2])
    second = all_reduce(1)
    next(second)
    total = acc[1] + back_part(1, 0)
    gate[1] = jnp.where(act[2] > 0, total, 0.0).astype(BF)
    for d in range(2):
        right_factor(0, bq_first, d, gate[d])
    loads[5].wait()
    wait_halo(1)
    for plane in (0, 3):
        vol[plane] = masked(vol, plane)
    pairs = []
    for a in range(3):
        grad_left(0, a, bq_first[...], vol[a : a + 2])
        pairs.append(pair_step(0, a))
        if a > 0:
            pair_add(0, a - 1, pairs[a - 1])
    for d in range(2):
        store_shifts(gv, d, gate[d])
    wait_halo(2)
    for plane in (0, 3):
        act[plane] = jnp.maximum(masked(act, plane), jnp.zeros((CELLS, C), BF))
    pair_add(0, 2, pairs[2])
    first = all_reduce(0)
    next(first)
    grad_step(1, act, cv, 1, 0)
    grad_step(1, act, cv, 1, 1)
    next(second)
    for i in range(2, 8):
        grad_step(1, act, cv, 1, i)
    next(first)
    second_copies = next(second)
    grad_step(1, act, cv, 1, 8)
    for i in range(0, 4):
        grad_step(0, vol, gv, 0, i)
    first_copies = next(first)
    for i in range(4, 9):
        grad_step(0, vol, gv, 0, i)

    eye = (
        lax.broadcasted_iota(jnp.int32, (RANK, RANK), 0)
        == lax.broadcasted_iota(jnp.int32, (RANK, RANK), 1)
    ).astype(F32)
    rows = lax.broadcasted_iota(jnp.int32, (RANK, 2 * RANK), 0)
    tables = [None, None]

    def eliminate(l, j0, j1):
        t = tables[l]
        for j in range(j0, j1):
            row = t[j : j + 1, :] * (1.0 / t[j : j + 1, j : j + 1])
            t = jnp.where(rows == j, row, t - t[:, j : j + 1] * row)
        tables[l] = t

    right_terms(1, second_copies)
    sum_second = right_reduce(1)
    next(sum_second)
    tables[1] = gram_table(1)
    eliminate(1, 0, 4)
    right_terms(0, first_copies, lambda: eliminate(1, 4, 14))
    sum_first = right_reduce(0)
    next(sum_first)
    next(sum_second)
    tables[0] = gram_table(0)
    eliminate(1, 14, 24)
    eliminate(0, 0, 10)
    next(sum_second)
    next(sum_first)
    eliminate(1, 24, 32)
    eliminate(0, 10, 23)
    next(sum_first)
    eliminate(0, 23, 32)
    next(sum_second)
    right = stacked_right(right_out[1])
    for k in range(27):
        part = slice(k * 256, (k + 1) * 256)
        tail[part, :] = (mat_second[part, :] - left_product(flat[1, k], right)).astype(BF)
    next(sum_first)
    for copy in pending:
        copy.wait_send()


def last_kernel(
    start_ref, mat_ref, left_ref, right_ref, tail_ref, err_hbm, sum_out, done, span, sems
):
    copies = [pltpu.make_async_copy(tail_ref, err_hbm.at[1], sems.at[0])]
    copies[0].start()
    right = stacked_right(right_ref[0])
    for i in range(9):
        for k in range(3 * i, 3 * i + 3):
            part = slice(k * 256, (k + 1) * 256)
            done[part, :] = (mat_ref[part, :] - left_product(left_ref[0, k], right)).astype(BF)
        part = pl.ds(768 * i, 768)
        copies.append(pltpu.make_async_copy(done.at[part], err_hbm.at[0, part], sems.at[1 + i]))
        copies[-1].start()
    start = start_ref[0]
    k = jnp.minimum(start // 256, 25)
    for l in range(2):
        right = stacked_right(right_ref[l])
        for j in range(2):
            span[l, 256 * j : 256 * (j + 1), :] = left_product(left_ref[l, k + j], right) * 128.0
        sum_out[l] = span[l, pl.ds(pl.multiple_of(start - k * 256, 8), ROWS // 32), :]
    for copy in copies:
        copy.wait()


def per_device(volume, pre_act, cotangent, kernel_second, q_start, error):
    def rows(x):
        return x.reshape(2, CELLS, C)

    hbm = pl.BlockSpec(memory_space=pltpu.HBM)
    vmem = pl.BlockSpec(memory_space=pltpu.VMEM)
    dma = pltpu.SemaphoreType.DMA
    V = pltpu.VMEM
    mat, left, right, tail = pl.pallas_call(
        main_kernel,
        out_shape=(
            V((ROWS, C), F32), V((2, 32, 2 * RANK, C), BF), V((2, RANK, C), F32), V((ROWS, C), BF),
        ),
        in_specs=[hbm] * 5 + [vmem],
        out_specs=(vmem, vmem, vmem, vmem),
        scratch_shapes=[
            V((4, CELLS, C), BF), V((4, CELLS, C), BF), V((4, CELLS, C), BF),
            V((27, C, C), BF), V((2, ROWS, C), BF), V((3, 4, PAD, C), BF), V((3, 2, PAD, C), BF),
            V((2, PAD, 6 * RANK), BF), V((4, PAD, 6 * RANK), BF),
            V((2, CELLS, C), F32), V((2, CELLS, C), BF), V((ROWS, C), F32),
            V((2, 2, 16, RANK, C), F32), V((2, 14, RANK, C), F32), V((2, 15, RANK, C), F32),
            V((2, 4, RANK, C), F32), V((2, 2, 16, RANK, C), F32),
            V((2, RANK, C), F32), V((2, 16, RANK, C), F32),
            dma((6,)), dma((3, 2)), dma((3, 2)), dma((2, 3)), dma((2, 3)), dma((2, 49)),
            dma((2, 49)), dma((2, 13)), dma((2, 13)),
        ],
        compiler_params=pltpu.CompilerParams(
            collective_id=0, has_side_effects=True, vmem_limit_bytes=MAIN_VMEM << 20
        ),
        name="main_kernel",
    )(
        rows(pre_act), rows(cotangent), rows(volume), kernel_second,
        error.reshape(2, ROWS, C), jnp.swapaxes(q_start, 1, 2),
    )
    start = (lax.axis_index("slab") * (ROWS // 32)).astype(jnp.int32).reshape(1)
    new_error, summed = pl.pallas_call(
        last_kernel,
        out_shape=(
            jax.ShapeDtypeStruct((2, ROWS, C), BF),
            jax.ShapeDtypeStruct((2, ROWS // 32, C), F32),
        ),
        in_specs=[pl.BlockSpec(memory_space=pltpu.SMEM), vmem, vmem, vmem, vmem],
        out_specs=(hbm, vmem),
        scratch_shapes=[V((ROWS, C), BF), V((2, 512, C), F32), dma((10,))],
        compiler_params=pltpu.CompilerParams(vmem_limit_bytes=LAST_VMEM << 20),
        name="last_kernel",
    )(start, mat, left, right, tail)
    return (summed, new_error.reshape(1, 1, 2, ROWS, C))


def solution(mesh):
    in_specs = (
        P("dp", "slab", None, None, None),
        P("dp", "slab", None, None, None),
        P("dp", "slab", None, None, None),
        P(),
        P(),
        P("dp", "slab", None, None, None),
    )
    out_specs = (P(None, "slab", None), P("dp", "slab", None, None, None))
    return jax.shard_map(
        per_device, mesh=mesh, in_specs=in_specs, out_specs=out_specs, check_vma=False
    )
```

```python
import functools

import jax
import jax.numpy as jnp
from jax import lax
from jax.experimental import pallas as pl
from jax.experimental.pallas import tpu as pltpu
from jax.sharding import PartitionSpec as P

BF, F32 = jnp.bfloat16, jnp.float32
MESH = pl.DeviceIdType.MESH
NT = (((1,), (1,)), ((), ()))
TN = (((0,), (0,)), ((), ()))
NN = (((1,), (0,)), ((), ()))
C, RANK, CELLS, WW, ROWS = 256, 32, 512, 32, 6912
PAD = CELLS + 2 * WW
MAIN_VMEM, LAST_VMEM = 46, 16


def mm(x, y, dims=NN):
    return lax.dot_general(x, y, dims, preferred_element_type=F32)


def split(x):
    hi = x.astype(BF)
    return hi, (x - hi.astype(F32)).astype(BF)


def precise(x, y, dims=NN):
    xh, xl = split(x)
    yh, yl = split(y)
    return mm(xh, yh, dims) + (mm(xh, yl, dims) + mm(xl, yh, dims))


def store_shifts(dst, plane, x):
    w = lax.broadcasted_iota(jnp.int32, (CELLS, C), 0) % WW
    wide = x.astype(F32)
    up = jnp.where(w == WW - 1, 0.0, pltpu.roll(wide, CELLS - 1, 0))
    down = jnp.where(w == 0, 0.0, pltpu.roll(wide, 1, 0))
    zero = jnp.zeros((WW, C), BF)
    for c, piece in enumerate((up.astype(BF), x, down.astype(BF))):
        dst[c, plane, 0:WW, :] = zero
        dst[c, plane, WW : WW + CELLS, :] = piece
        dst[c, plane, WW + CELLS : PAD, :] = zero


class Places:
    def __init__(self):
        self.y = lax.axis_index("dp")
        self.s = lax.axis_index("slab")
        self.x = self.s // 8
        self.z = (self.s // 2) % 4
        self.core = self.s % 2

    def at(self, dy, dx, dz, dcore=0):
        y = (self.y + dy) % 4
        x = (self.x + dx) % 4
        z = (self.z + dz) % 4
        core = (self.core + dcore) % 2
        return {"dp": y, "slab": x * 8 + z * 2 + core}

    def slab(self, step):
        return {"dp": self.y, "slab": (self.s + step + 32) % 32}


def left_product(both, right):
    return mm(jnp.concatenate([both[:RANK], both], 0), right, TN) * (1.0 / 128)


def stacked_right(right):
    hi, lo = split(right)
    return jnp.concatenate([lo, hi, hi], 0)


def main_kernel(
    pre_hbm, cot_hbm, vol_hbm, ker_hbm, err_hbm, qt_ref,
    mat_first, flat, right_out, tail,
    act, cot, vol, ker, err, cv, gv, bq_first, bq_second, acc, gate, mat_second, send, r0, r1, r2, fin,
    srcv, sall, local_sem, halo_send, halo_recv, pair_send, pair_recv, ar_send, ar_recv,
    s_send, s_recv,
):
    me = Places()
    s, core = me.s, me.core
    one = 1 - core

    loads = []
    for i, (src, dst) in enumerate(
        (
            (cot_hbm, cot.at[1:3]),
            (pre_hbm, act.at[1:3]),
            (err_hbm.at[1], err.at[1]),
            (ker_hbm, ker),
            (err_hbm.at[0], err.at[0]),
            (vol_hbm, vol.at[1:3]),
        )
    ):
        copy = pltpu.make_async_copy(src, dst, local_sem.at[i])
        copy.start()
        loads.append(copy)

    barrier = pltpu.get_barrier_semaphore()
    peers = [me.slab(-1), me.slab(1)]
    for i in range(1, 4):
        peers += [me.at(i, 0, 0), me.at(0, i, 0)]
        for j in range(1, 4):
            peers += [me.at(i, j, 0), me.at(i * one, i * core, j)]
    peers += [me.at(0, 0, i // 2, i % 2) for i in range(1, 8)]
    for peer in peers:
        pl.semaphore_signal(barrier, inc=1, device_id=peer, device_id_type=MESH)
    halos = []

    def send_halos():
        for i, (src, dst) in enumerate(((cot_hbm, cot), (vol_hbm, vol), (pre_hbm, act))):
            pair = []
            for j, (plane, slot, step) in enumerate(((1, 0, 1), (0, 3, -1))):
                copy = pltpu.make_async_remote_copy(
                    src_ref=src.at[plane], dst_ref=dst.at[slot],
                    send_sem=halo_send.at[i, j], recv_sem=halo_recv.at[i, j],
                    device_id=me.slab(step), device_id_type=MESH,
                )
                copy.start()
                pair.append(copy)
            halos.append(pair)

    def wait_halo(i):
        for copy in halos[i]:
            copy.wait()

    def masked(ref, plane):
        if plane == 0:
            return jnp.where(s > 0, ref[0], jnp.zeros((CELLS, C), BF))
        if plane == 3:
            return jnp.where(s < 31, ref[3], jnp.zeros((CELLS, C), BF))
        return ref[plane]

    q2 = [jnp.concatenate(split(qt_ref[l]), 0) for l in range(2)]

    def error_left(l):
        for k in range(27):
            t = mm(q2[l], err[l, k * 256 : (k + 1) * 256, :], NT)
            send[l, k % 2, k // 2] = t[:RANK] + t[RANK:]
        for k in range(27, 32):
            send[l, k % 2, k // 2] = jnp.zeros((RANK, C), F32)

    def error_half(l, hand, add):
        for t in range(14):
            k = 2 * t + hand
            row = pl.multiple_of(jnp.minimum(k, 26) * 256, 256)
            value = mm(q2[l], err[l, pl.ds(row, 256), :], NT)
            value = jnp.where(k < 27, value[:RANK] + value[RANK:], 0.0)
            send[l, hand, t] = send[l, hand, t] + value if add else value

    def right_factor(l, dst, d, x):
        t = mm(x, q2[l], NT)
        t = t[:, :RANK] + t[:, RANK:]
        w = lax.broadcasted_iota(jnp.int32, (CELLS, RANK), 0) % WW
        up = jnp.where(w == WW - 1, 0.0, pltpu.roll(t, CELLS - 1, 0))
        down = jnp.where(w == 0, 0.0, pltpu.roll(t, 1, 0))
        zero = jnp.zeros((WW, 6 * RANK), BF)
        dst[d, 0:WW, :] = zero
        dst[d, WW : WW + CELLS, :] = jnp.concatenate([*split(up), *split(t), *split(down)], 1)
        dst[d, WW + CELLS : PAD, :] = zero

    def grad_left(l, a, factor, planes):
        size = planes.shape[0] * CELLS
        for b in range(3):
            r = (2 - b) * WW
            x = factor[:, r : r + CELLS, :].reshape(size, 6 * RANK)
            t = mm(x, planes[...].reshape(size, C), TN)
            for c in range(3):
                k = 9 * a + 3 * b + c
                piece = t[64 * c : 64 * c + 32] + t[64 * c + 32 : 64 * c + 64]
                send[l, k % 2, k // 2] = send[l, k % 2, k // 2] + piece

    near = [(min(i, 4 - i) + min(j, 4 - j), i, j) for i in range(4) for j in range(4)]
    others = [(i, j) for d, i, j in sorted(near, reverse=True) if d > 0]

    def plane_index(l, hand, i, j):
        if l == 1:
            return (me.y + i) % 4 * 4 + (me.x + j) % 4
        return (me.y * (1 - hand) + me.x * hand + i) % 4 * 4 + (me.z + j) % 4

    def plane_peer(l, i, j):
        return me.at(i, j, 0) if l == 1 else me.at(i * one, i * core, j)

    def axis_index(l):
        return me.z if l == 1 else me.x * one + me.y * core

    def axis_peer(l, i):
        return me.at(0, 0, i) if l == 1 else me.at(i * core, i * one, 0)

    pending, forwards = [], {}

    def push(src, dst, sems, l, n, peer):
        copy = pltpu.make_async_remote_copy(
            src_ref=src, dst_ref=dst, send_sem=sems[0].at[l, n], recv_sem=sems[1].at[l, n],
            device_id=peer, device_id_type=MESH,
        )
        copy.start()
        pending.append(copy)
        return copy

    ar_sems = (ar_send, ar_recv)
    pair_sems = (pair_send, pair_recv)
    bounds = (((0, 4), (4, 9), (9, 14)), ((0, 5), (5, 9), (9, 14)))

    def settle():
        for copy in pending:
            copy.wait_send()
        pending.clear()

    def pair_step(l, n):
        low, high = bounds[l][n]
        part = pl.ds(low, high - low)
        return push(
            send.at[l, one, part], r0.at[l, part], pair_sems, l, n, me.at(0, 0, 0, 1)
        )

    def pair_add(l, n, copy):
        copy.wait_recv()
        for t in range(*bounds[l][n]):
            send[l, core, t] = send[l, core, t] + r0[l, t]

    def all_reduce(l):
        here = plane_index(l, core, 0, 0)
        copies = [
            push(
                send.at[l, core, plane_index(l, core, i, j)], r1.at[l, n],
                ar_sems, l, n, plane_peer(l, i, j),
            )
            for n, (i, j) in enumerate(others)
        ]
        yield
        total = send[l, core, here]
        for n in range(14, -1, -1):
            copies[n].wait_recv()
            total = total + r1[l, n]
        i3 = axis_index(l)
        r2[l, i3] = total
        copies = [
            push(r2.at[l, i3], r2.at[l, i3], ar_sems, l, 14 + i, axis_peer(l, i))
            for i in range(1, 4)
        ]
        yield
        for copy in copies:
            copy.wait_recv()
        fin[l, core, here] = (r2[l, 0] + r2[l, 1]) + (r2[l, 2] + r2[l, 3])
        copies = [
            push(
                fin.at[l, core, here], fin.at[l, core, here], ar_sems, l, 18 + n,
                plane_peer(l, i, j),
            )
            for n, (i, j) in enumerate(others)
        ]
        forward(l, 0, 0, 0)
        yield copies

    def forward(l, n, i, j):
        slot = fin.at[l, core, plane_index(l, core, i, j)]
        forwards[l, n] = push(slot, slot, ar_sems, l, 33 + n, me.at(0, 0, 0, 1))

    def right_tap(l, hand, tap, sums):
        mat = mat_first if l == 0 else mat_second
        k = 2 * tap + hand
        row = pl.multiple_of(jnp.minimum(k, 26) * 256, 256)
        mh, ml = split(mat[pl.ds(row, 256), :])
        both = jnp.concatenate(split(fin[l, hand, tap]), 0)
        flat[l, k] = both
        t = mm(both, mh)
        return sums + (t[:RANK] + (t[RANK:] + mm(both[:RANK], ml)))

    def gram_table(l):
        gram = jnp.zeros((2 * RANK, 2 * RANK), F32)
        for k in range(27):
            gram = gram + mm(flat[l, k], flat[l, k], NT)
        gram = (gram[:RANK, :RANK] + gram[RANK:, RANK:]) + (
            gram[:RANK, RANK:] + gram[RANK:, :RANK]
        )
        return jnp.concatenate([gram, eye], 1)

    def right_terms(l, copies, middle=lambda: None):
        sums = jnp.zeros((RANK, C), F32)
        done = [(0, 0)]
        for low, high in ((7, 15), (0, 7)):
            for n in range(high - 1, low - 1, -1):
                sender = others[n]
                source = (-sender[0]) % 4, (-sender[1]) % 4
                copies[n].wait_recv()
                forward(l, 1 + n, *source)
                done.append(source)
            for i, j in done:
                sums = right_tap(l, core, plane_index(l, core, i, j), sums)
            done = []
        for n in [0] + list(range(15, 0, -1)):
            forwards[l, n].wait_recv()
        middle()
        for t in range(14):
            sums = right_tap(l, one, t, sums)
        srcv[l] = sums

    def right_reduce(l):
        s_sems = (s_send, s_recv)
        mine = srcv[l]
        for n, (index, step) in enumerate(((me.y, (1, 0, 0)), (me.x, (0, 1, 0)))):
            slot = 4 * n + index
            sall[l, slot] = mine
            copies = [
                push(
                    sall.at[l, slot], sall.at[l, slot], s_sems, l, 3 * n + i - 1,
                    me.at(*(i * v for v in step)),
                )
                for i in range(1, 4)
            ]
            yield
            for copy in copies:
                copy.wait_recv()
            mine = (sall[l, 4 * n] + sall[l, 4 * n + 1]) + (sall[l, 4 * n + 2] + sall[l, 4 * n + 3])
        slot = 8 + 2 * me.z + core
        sall[l, slot] = mine
        copies = [
            push(sall.at[l, slot], sall.at[l, slot], s_sems, l, 5 + i, me.at(0, 0, i // 2, i % 2))
            for i in range(1, 8)
        ]
        yield
        for copy in copies:
            copy.wait_recv()
        total = [sall[l, 8 + 2 * i] + sall[l, 9 + 2 * i] for i in range(4)]
        right_out[l] = precise(tables[l][:, RANK:], (total[0] + total[1]) + (total[2] + total[3]))
        yield

    def grad_step(l, planes, source, first, i):
        b, c = i // 3, i % 3
        r = (2 - b) * WW
        right = source[c, first : first + 2, r : r + CELLS, :].reshape(2 * CELLS, C)
        for a in range(3):
            rows = slice((9 * a + i) * 256, (9 * a + i + 1) * 256)
            g = mm(planes[a : a + 2].reshape(2 * CELLS, C), right, TN)
            mat = mat_first if l == 0 else mat_second
            mat[rows, :] = g + err[l, rows, :].astype(F32)

    def back_part(d, a):
        x = jnp.concatenate(
            [
                cv[c, d + 2 - a, (2 - b) * WW : (2 - b) * WW + CELLS, :]
                for b in range(3)
                for c in range(3)
            ],
            1,
        )
        w = jnp.concatenate([ker[9 * a + i] for i in range(9)], 1)
        return mm(x, w, NT)

    loads[0].wait()
    for plane in (1, 2):
        right_factor(1, bq_second, plane, cot[plane])
    loads[1].wait()
    for plane in (1, 2):
        act[plane] = jnp.maximum(act[plane], jnp.zeros((CELLS, C), BF))
    loads[2].wait()
    error_left(1)
    grad_left(1, 1, bq_second[1:3], act[1:3])
    pl.semaphore_wait(barrier, len(peers))
    send_halos()
    pairs = {1: pair_step(1, 1)}
    grad_left(1, 0, bq_second[2:3], act[1:2])
    grad_left(1, 2, bq_second[1:2], act[2:3])
    for plane in (1, 2):
        store_shifts(cv, plane, cot[plane])
    loads[3].wait()
    acc[0] = back_part(0, 0) + back_part(0, 1)
    acc[1] = back_part(1, 1) + back_part(1, 2)
    pair_add(1, 1, pairs[1])
    loads[4].wait()
    error_half(0, one, False)
    for t in range(16):
        send[0, core, t] = jnp.zeros((RANK, C), F32)
    wait_halo(0)
    for plane in (0, 3):
        right_factor(1, bq_second, plane, masked(cot, plane))
    grad_left(1, 0, bq_second[3:4], act[2:3])
    pairs[0] = pair_step(1, 0)
    grad_left(1, 2, bq_second[0:1], act[1:2])
    pairs[2] = pair_step(1, 2)
    for plane in (0, 3):
        store_shifts(cv, plane, masked(cot, plane))
    total = acc[0] + back_part(0, 2)
    gate[0] = jnp.where(act[1] > 0, total, 0.0).astype(BF)
    pair_add(1, 0, pairs[0])
    pair_add(1, 2, pairs[2])
    second = all_reduce(1)
    next(second)
    total = acc[1] + back_part(1, 0)
    gate[1] = jnp.where(act[2] > 0, total, 0.0).astype(BF)
    for d in range(2):
        right_factor(0, bq_first, d, gate[d])
    loads[5].wait()
    wait_halo(1)
    for plane in (0, 3):
        vol[plane] = masked(vol, plane)
    pairs = []
    for a in range(3):
        grad_left(0, a, bq_first[...], vol[a : a + 2])
        pairs.append(pair_step(0, a))
        if a > 0:
            pair_add(0, a - 1, pairs[a - 1])
    error_half(0, core, True)
    pair_add(0, 2, pairs[2])
    first = all_reduce(0)
    next(first)
    for d in range(2):
        store_shifts(gv, d, gate[d])
    wait_halo(2)
    for plane in (0, 3):
        act[plane] = jnp.maximum(masked(act, plane), jnp.zeros((CELLS, C), BF))
    grad_step(1, act, cv, 1, 0)
    grad_step(1, act, cv, 1, 1)
    next(second)
    for i in range(2, 8):
        grad_step(1, act, cv, 1, i)
    next(first)
    second_copies = next(second)
    grad_step(1, act, cv, 1, 8)
    for i in range(0, 4):
        grad_step(0, vol, gv, 0, i)
    first_copies = next(first)
    for i in range(4, 9):
        grad_step(0, vol, gv, 0, i)

    eye = (
        lax.broadcasted_iota(jnp.int32, (RANK, RANK), 0)
        == lax.broadcasted_iota(jnp.int32, (RANK, RANK), 1)
    ).astype(F32)
    rows = lax.broadcasted_iota(jnp.int32, (RANK, 2 * RANK), 0)
    tables = [None, None]

    def eliminate(l, j0, j1):
        t = tables[l]
        for j in range(j0, j1):
            row = t[j : j + 1, :] * (1.0 / t[j : j + 1, j : j + 1])
            t = jnp.where(rows == j, row, t - t[:, j : j + 1] * row)
        tables[l] = t

    right_terms(1, second_copies)
    sum_second = right_reduce(1)
    next(sum_second)
    tables[1] = gram_table(1)
    eliminate(1, 0, 4)
    right_terms(0, first_copies, lambda: eliminate(1, 4, 14))
    sum_first = right_reduce(0)
    next(sum_first)
    next(sum_second)
    tables[0] = gram_table(0)
    eliminate(1, 14, 24)
    eliminate(0, 0, 10)
    next(sum_second)
    next(sum_first)
    eliminate(1, 24, 32)
    eliminate(0, 10, 23)
    settle()
    next(sum_first)
    eliminate(0, 23, 32)
    next(sum_second)
    right = stacked_right(right_out[1])
    for k in range(27):
        part = slice(k * 256, (k + 1) * 256)
        tail[part, :] = (mat_second[part, :] - left_product(flat[1, k], right)).astype(BF)
    next(sum_first)
    settle()


def last_kernel(
    start_ref, mat_ref, left_ref, right_ref, tail_ref, err_hbm, sum_hbm, done, span, sems
):
    copies = [pltpu.make_async_copy(tail_ref, err_hbm.at[1], sems.at[0])]
    copies[0].start()
    start = start_ref[0]
    k = jnp.minimum(start // 256, 25)
    part = pl.ds(pl.multiple_of(start - k * 256, 8), ROWS // 32)
    for l in range(2):
        right = stacked_right(right_ref[l])
        for j in range(2):
            span[l, 256 * j : 256 * (j + 1), :] = left_product(left_ref[l, k + j], right) * 128.0
        copies.append(pltpu.make_async_copy(span.at[l, part], sum_hbm.at[l], sems.at[1 + l]))
        copies[-1].start()
    right = stacked_right(right_ref[0])
    for i in range(9):
        for k in range(3 * i, 3 * i + 3):
            part = slice(k * 256, (k + 1) * 256)
            done[part, :] = (mat_ref[part, :] - left_product(left_ref[0, k], right)).astype(BF)
        part = pl.ds(768 * i, 768)
        copies.append(pltpu.make_async_copy(done.at[part], err_hbm.at[0, part], sems.at[3 + i]))
        copies[-1].start()
    for copy in copies:
        copy.wait()


def per_device(volume, pre_act, cotangent, kernel_second, q_start, error):
    def rows(x):
        return x.reshape(2, CELLS, C)

    hbm = pl.BlockSpec(memory_space=pltpu.HBM)
    vmem = pl.BlockSpec(memory_space=pltpu.VMEM)
    dma = pltpu.SemaphoreType.DMA
    V = pltpu.VMEM
    mat, left, right, tail = pl.pallas_call(
        main_kernel,
        out_shape=(
            V((ROWS, C), F32), V((2, 32, 2 * RANK, C), BF), V((2, RANK, C), F32), V((ROWS, C), BF),
        ),
        in_specs=[hbm] * 5 + [vmem],
        out_specs=(vmem, vmem, vmem, vmem),
        scratch_shapes=[
            V((4, CELLS, C), BF), V((4, CELLS, C), BF), V((4, CELLS, C), BF),
            V((27, C, C), BF), V((2, ROWS, C), BF), V((3, 4, PAD, C), BF), V((3, 2, PAD, C), BF),
            V((2, PAD, 6 * RANK), BF), V((4, PAD, 6 * RANK), BF),
            V((2, CELLS, C), F32), V((2, CELLS, C), BF), V((ROWS, C), F32),
            V((2, 2, 16, RANK, C), F32), V((2, 14, RANK, C), F32), V((2, 15, RANK, C), F32),
            V((2, 4, RANK, C), F32), V((2, 2, 16, RANK, C), F32),
            V((2, RANK, C), F32), V((2, 16, RANK, C), F32),
            dma((6,)), dma((3, 2)), dma((3, 2)), dma((2, 3)), dma((2, 3)), dma((2, 49)),
            dma((2, 49)), dma((2, 13)), dma((2, 13)),
        ],
        compiler_params=pltpu.CompilerParams(
            collective_id=0, has_side_effects=True, vmem_limit_bytes=MAIN_VMEM << 20
        ),
        name="main_kernel",
    )(
        rows(pre_act), rows(cotangent), rows(volume), kernel_second,
        error.reshape(2, ROWS, C), jnp.swapaxes(q_start, 1, 2),
    )
    start = (lax.axis_index("slab") * (ROWS // 32)).astype(jnp.int32).reshape(1)
    new_error, summed = pl.pallas_call(
        last_kernel,
        out_shape=(
            jax.ShapeDtypeStruct((2, ROWS, C), BF),
            jax.ShapeDtypeStruct((2, ROWS // 32, C), F32),
        ),
        in_specs=[pl.BlockSpec(memory_space=pltpu.SMEM), vmem, vmem, vmem, vmem],
        out_specs=(hbm, hbm),
        scratch_shapes=[V((ROWS, C), BF), V((2, 512, C), F32), dma((12,))],
        compiler_params=pltpu.CompilerParams(vmem_limit_bytes=LAST_VMEM << 20),
        name="last_kernel",
    )(start, mat, left, right, tail)
    return (summed, new_error.reshape(1, 1, 2, ROWS, C))


def solution(mesh):
    in_specs = (
        P("dp", "slab", None, None, None),
        P("dp", "slab", None, None, None),
        P("dp", "slab", None, None, None),
        P(),
        P(),
        P("dp", "slab", None, None, None),
    )
    out_specs = (P(None, "slab", None), P("dp", "slab", None, None, None))
    return jax.shard_map(
        per_device, mesh=mesh, in_specs=in_specs, out_specs=out_specs, check_vma=False
    )
```

```python
import functools

import jax
import jax.numpy as jnp
from jax import lax
from jax.experimental import pallas as pl
from jax.experimental.pallas import tpu as pltpu
from jax.sharding import PartitionSpec as P

BF, F32 = jnp.bfloat16, jnp.float32
MESH = pl.DeviceIdType.MESH
NT = (((1,), (1,)), ((), ()))
TN = (((0,), (0,)), ((), ()))
NN = (((1,), (0,)), ((), ()))
C, RANK, CELLS, WW, ROWS = 256, 32, 512, 32, 6912
PAD = CELLS + 2 * WW
MAIN_VMEM, LAST_VMEM = 46, 16


def mm(x, y, dims=NN):
    return lax.dot_general(x, y, dims, preferred_element_type=F32)


def split(x):
    hi = x.astype(BF)
    return hi, (x - hi.astype(F32)).astype(BF)


def precise(x, y, dims=NN):
    xh, xl = split(x)
    yh, yl = split(y)
    return mm(xh, yh, dims) + (mm(xh, yl, dims) + mm(xl, yh, dims))


def store_center(dst, plane, x):
    zero = jnp.zeros((WW, C), BF)
    dst[1, plane, 0:WW, :] = zero
    dst[1, plane, WW : WW + CELLS, :] = x
    dst[1, plane, WW + CELLS : PAD, :] = zero


def store_shifts(dst, plane, x):
    w = lax.broadcasted_iota(jnp.int32, (CELLS, C), 0) % WW
    wide = x.astype(F32)
    up = jnp.where(w == WW - 1, 0.0, pltpu.roll(wide, CELLS - 1, 0))
    down = jnp.where(w == 0, 0.0, pltpu.roll(wide, 1, 0))
    zero = jnp.zeros((WW, C), BF)
    for c, piece in enumerate((up.astype(BF), x, down.astype(BF))):
        dst[c, plane, 0:WW, :] = zero
        dst[c, plane, WW : WW + CELLS, :] = piece
        dst[c, plane, WW + CELLS : PAD, :] = zero


class Places:
    def __init__(self):
        self.y = lax.axis_index("dp")
        self.s = lax.axis_index("slab")
        self.x = self.s // 8
        self.z = (self.s // 2) % 4
        self.core = self.s % 2

    def at(self, dy, dx, dz, dcore=0):
        y = (self.y + dy) % 4
        x = (self.x + dx) % 4
        z = (self.z + dz) % 4
        core = (self.core + dcore) % 2
        return {"dp": y, "slab": x * 8 + z * 2 + core}

    def slab(self, step):
        return {"dp": self.y, "slab": (self.s + step + 32) % 32}


def left_product(both, right):
    return mm(jnp.concatenate([both[:RANK], both], 0), right, TN) * (1.0 / 128)


def stacked_right(right):
    hi, lo = split(right)
    return jnp.concatenate([lo, hi, hi], 0)


def main_kernel(
    pre_hbm, cot_hbm, vol_hbm, ker_hbm, err_hbm, qt_ref,
    mat_first, flat, right_out, tail,
    act, cot, vol, ker, err, cv, gv, bq_first, bq_second, acc, gate, mat_second, send, r0, r1, r2, fin,
    srcv, sall, local_sem, halo_send, halo_recv, pair_send, pair_recv, ar_send, ar_recv,
    s_send, s_recv,
):
    me = Places()
    s, core = me.s, me.core
    one = 1 - core

    loads = []
    for i, (src, dst) in enumerate(
        (
            (cot_hbm, cot.at[1:3]),
            (pre_hbm, act.at[1:3]),
            (err_hbm.at[1], err.at[1]),
            (ker_hbm, ker),
            (err_hbm.at[0], err.at[0]),
            (vol_hbm, vol.at[1:3]),
        )
    ):
        copy = pltpu.make_async_copy(src, dst, local_sem.at[i])
        copy.start()
        loads.append(copy)

    barrier = pltpu.get_barrier_semaphore()
    peers = [me.slab(-1), me.slab(1)]
    for i in range(1, 4):
        peers += [me.at(i, 0, 0), me.at(0, i, 0)]
        for j in range(1, 4):
            peers += [me.at(i, j, 0), me.at(i * one, i * core, j)]
    peers += [me.at(0, 0, i // 2, i % 2) for i in range(1, 8)]
    for peer in peers:
        pl.semaphore_signal(barrier, inc=1, device_id=peer, device_id_type=MESH)
    halos = []

    def send_halos():
        for i, (src, dst) in enumerate(((cot_hbm, cot), (vol_hbm, vol), (pre_hbm, act))):
            pair = []
            for j, (plane, slot, step) in enumerate(((1, 0, 1), (0, 3, -1))):
                copy = pltpu.make_async_remote_copy(
                    src_ref=src.at[plane], dst_ref=dst.at[slot],
                    send_sem=halo_send.at[i, j], recv_sem=halo_recv.at[i, j],
                    device_id=me.slab(step), device_id_type=MESH,
                )
                copy.start()
                pair.append(copy)
            halos.append(pair)

    def wait_halo(i):
        for copy in halos[i]:
            copy.wait()

    def masked(ref, plane):
        if plane == 0:
            return jnp.where(s > 0, ref[0], jnp.zeros((CELLS, C), BF))
        if plane == 3:
            return jnp.where(s < 31, ref[3], jnp.zeros((CELLS, C), BF))
        return ref[plane]

    q2 = [jnp.concatenate(split(qt_ref[l]), 0) for l in range(2)]

    def error_left(l):
        for k in range(27):
            t = mm(q2[l], err[l, k * 256 : (k + 1) * 256, :], NT)
            send[l, k % 2, k // 2] = t[:RANK] + t[RANK:]
        for k in range(27, 32):
            send[l, k % 2, k // 2] = jnp.zeros((RANK, C), F32)

    def error_half(l, hand, add):
        for t in range(14):
            k = 2 * t + hand
            row = pl.multiple_of(jnp.minimum(k, 26) * 256, 256)
            value = mm(q2[l], err[l, pl.ds(row, 256), :], NT)
            value = jnp.where(k < 27, value[:RANK] + value[RANK:], 0.0)
            send[l, hand, t] = send[l, hand, t] + value if add else value

    def right_factor(l, dst, d, x):
        t = mm(x, q2[l], NT)
        t = t[:, :RANK] + t[:, RANK:]
        w = lax.broadcasted_iota(jnp.int32, (CELLS, RANK), 0) % WW
        up = jnp.where(w == WW - 1, 0.0, pltpu.roll(t, CELLS - 1, 0))
        down = jnp.where(w == 0, 0.0, pltpu.roll(t, 1, 0))
        zero = jnp.zeros((WW, 6 * RANK), BF)
        dst[d, 0:WW, :] = zero
        dst[d, WW : WW + CELLS, :] = jnp.concatenate([*split(up), *split(t), *split(down)], 1)
        dst[d, WW + CELLS : PAD, :] = zero

    def grad_left(l, a, factor, planes):
        size = planes.shape[0] * CELLS
        for b in range(3):
            r = (2 - b) * WW
            x = factor[:, r : r + CELLS, :].reshape(size, 6 * RANK)
            t = mm(x, planes[...].reshape(size, C), TN)
            for c in range(3):
                k = 9 * a + 3 * b + c
                piece = t[64 * c : 64 * c + 32] + t[64 * c + 32 : 64 * c + 64]
                send[l, k % 2, k // 2] = send[l, k % 2, k // 2] + piece

    near = [(min(i, 4 - i) + min(j, 4 - j), i, j) for i in range(4) for j in range(4)]
    others = [(i, j) for d, i, j in sorted(near, reverse=True) if d > 0]

    def plane_index(l, hand, i, j):
        if l == 1:
            return (me.y + i) % 4 * 4 + (me.x + j) % 4
        return (me.y * (1 - hand) + me.x * hand + i) % 4 * 4 + (me.z + j) % 4

    def plane_peer(l, i, j):
        return me.at(i, j, 0) if l == 1 else me.at(i * one, i * core, j)

    def axis_index(l):
        return me.z if l == 1 else me.x * one + me.y * core

    def axis_peer(l, i):
        return me.at(0, 0, i) if l == 1 else me.at(i * core, i * one, 0)

    pending, forwards = [], {}

    def push(src, dst, sems, l, n, peer):
        copy = pltpu.make_async_remote_copy(
            src_ref=src, dst_ref=dst, send_sem=sems[0].at[l, n], recv_sem=sems[1].at[l, n],
            device_id=peer, device_id_type=MESH,
        )
        copy.start()
        pending.append(copy)
        return copy

    ar_sems = (ar_send, ar_recv)
    pair_sems = (pair_send, pair_recv)
    bounds = (((0, 4), (4, 9), (9, 14)), ((0, 5), (5, 9), (9, 14)))

    def settle():
        for copy in pending:
            copy.wait_send()
        pending.clear()

    def pair_step(l, n):
        low, high = bounds[l][n]
        part = pl.ds(low, high - low)
        return push(
            send.at[l, one, part], r0.at[l, part], pair_sems, l, n, me.at(0, 0, 0, 1)
        )

    def pair_add(l, n, copy):
        copy.wait_recv()
        for t in range(*bounds[l][n]):
            send[l, core, t] = send[l, core, t] + r0[l, t]

    def all_reduce(l):
        here = plane_index(l, core, 0, 0)
        copies = [
            push(
                send.at[l, core, plane_index(l, core, i, j)], r1.at[l, n],
                ar_sems, l, n, plane_peer(l, i, j),
            )
            for n, (i, j) in enumerate(others)
        ]
        yield
        total = send[l, core, here]
        for n in range(14, -1, -1):
            copies[n].wait_recv()
            total = total + r1[l, n]
        i3 = axis_index(l)
        r2[l, i3] = total
        copies = [
            push(r2.at[l, i3], r2.at[l, i3], ar_sems, l, 14 + i, axis_peer(l, i))
            for i in range(1, 4)
        ]
        yield
        for copy in copies:
            copy.wait_recv()
        fin[l, core, here] = (r2[l, 0] + r2[l, 1]) + (r2[l, 2] + r2[l, 3])
        copies = [
            push(
                fin.at[l, core, here], fin.at[l, core, here], ar_sems, l, 18 + n,
                plane_peer(l, i, j),
            )
            for n, (i, j) in enumerate(others)
        ]
        forward(l, 0, 0, 0)
        yield copies

    def forward(l, n, i, j):
        slot = fin.at[l, core, plane_index(l, core, i, j)]
        forwards[l, n] = push(slot, slot, ar_sems, l, 33 + n, me.at(0, 0, 0, 1))

    def right_tap(l, hand, tap, sums):
        mat = mat_first if l == 0 else mat_second
        k = 2 * tap + hand
        row = pl.multiple_of(jnp.minimum(k, 26) * 256, 256)
        mh, ml = split(mat[pl.ds(row, 256), :])
        both = jnp.concatenate(split(fin[l, hand, tap]), 0)
        flat[l, k] = both
        t = mm(both, mh)
        return sums + (t[:RANK] + (t[RANK:] + mm(both[:RANK], ml)))

    def gram_table(l):
        gram = jnp.zeros((2 * RANK, 2 * RANK), F32)
        for k in range(27):
            gram = gram + mm(flat[l, k], flat[l, k], NT)
        gram = (gram[:RANK, :RANK] + gram[RANK:, RANK:]) + (
            gram[:RANK, RANK:] + gram[RANK:, :RANK]
        )
        return jnp.concatenate([gram, eye], 1)

    def right_terms(l, copies, middle=lambda: None):
        sums = jnp.zeros((RANK, C), F32)
        done = [(0, 0)]
        for low, high in ((7, 15), (0, 7)):
            for n in range(high - 1, low - 1, -1):
                sender = others[n]
                source = (-sender[0]) % 4, (-sender[1]) % 4
                copies[n].wait_recv()
                forward(l, 1 + n, *source)
                done.append(source)
            for i, j in done:
                sums = right_tap(l, core, plane_index(l, core, i, j), sums)
            done = []
        for n in [0] + list(range(15, 0, -1)):
            forwards[l, n].wait_recv()
        middle()
        for t in range(14):
            sums = right_tap(l, one, t, sums)
        srcv[l] = sums

    def right_reduce(l):
        s_sems = (s_send, s_recv)
        mine = srcv[l]
        for n, (index, step) in enumerate(((me.y, (1, 0, 0)), (me.x, (0, 1, 0)))):
            slot = 4 * n + index
            sall[l, slot] = mine
            copies = [
                push(
                    sall.at[l, slot], sall.at[l, slot], s_sems, l, 3 * n + i - 1,
                    me.at(*(i * v for v in step)),
                )
                for i in range(1, 4)
            ]
            yield
            for copy in copies:
                copy.wait_recv()
            mine = (sall[l, 4 * n] + sall[l, 4 * n + 1]) + (sall[l, 4 * n + 2] + sall[l, 4 * n + 3])
        slot = 8 + 2 * me.z + core
        sall[l, slot] = mine
        copies = [
            push(sall.at[l, slot], sall.at[l, slot], s_sems, l, 5 + i, me.at(0, 0, i // 2, i % 2))
            for i in range(1, 8)
        ]
        yield
        for copy in copies:
            copy.wait_recv()
        total = [sall[l, 8 + 2 * i] + sall[l, 9 + 2 * i] for i in range(4)]
        right_out[l] = precise(tables[l][:, RANK:], (total[0] + total[1]) + (total[2] + total[3]))
        yield

    def grad_step(l, planes, source, first, i):
        b, c = i // 3, i % 3
        r = (2 - b) * WW
        right = source[c, first : first + 2, r : r + CELLS, :].reshape(2 * CELLS, C)
        for a in range(3):
            rows = slice((9 * a + i) * 256, (9 * a + i + 1) * 256)
            g = mm(planes[a : a + 2].reshape(2 * CELLS, C), right, TN)
            mat = mat_first if l == 0 else mat_second
            mat[rows, :] = g + err[l, rows, :].astype(F32)

    def back_part(d, a, c):
        x = jnp.concatenate(
            [cv[1, d + 2 - a, (2 - b) * WW : (2 - b) * WW + CELLS, :] for b in range(3)], 1
        )
        return mm(x, jnp.concatenate([ker[9 * a + 3 * b + c] for b in range(3)], 1), NT)

    def back_done(d):
        parts = [acc[d, c] + back_part(d, 2 - 2 * d, c) for c in range(3)]
        w = lax.broadcasted_iota(jnp.int32, (CELLS, C), 0) % WW
        up = jnp.where(w == WW - 1, 0.0, pltpu.roll(parts[0], CELLS - 1, 0))
        down = jnp.where(w == 0, 0.0, pltpu.roll(parts[2], 1, 0))
        total = parts[1] + up + down
        gate[d] = jnp.where(act[1 + d] > 0, total, 0.0).astype(BF)

    loads[0].wait()
    for plane in (1, 2):
        right_factor(1, bq_second, plane, cot[plane])
    loads[1].wait()
    for plane in (1, 2):
        act[plane] = jnp.maximum(act[plane], jnp.zeros((CELLS, C), BF))
    loads[2].wait()
    error_left(1)
    grad_left(1, 1, bq_second[1:3], act[1:3])
    pl.semaphore_wait(barrier, len(peers))
    send_halos()
    pairs = {1: pair_step(1, 1)}
    grad_left(1, 0, bq_second[2:3], act[1:2])
    grad_left(1, 2, bq_second[1:2], act[2:3])
    for plane in (1, 2):
        store_center(cv, plane, cot[plane])
    loads[3].wait()
    for c in range(3):
        acc[0, c] = back_part(0, 0, c) + back_part(0, 1, c)
        acc[1, c] = back_part(1, 1, c) + back_part(1, 2, c)
    pair_add(1, 1, pairs[1])
    loads[4].wait()
    error_half(0, one, False)
    for t in range(16):
        send[0, core, t] = jnp.zeros((RANK, C), F32)
    wait_halo(0)
    for plane in (0, 3):
        right_factor(1, bq_second, plane, masked(cot, plane))
    grad_left(1, 0, bq_second[3:4], act[2:3])
    pairs[0] = pair_step(1, 0)
    grad_left(1, 2, bq_second[0:1], act[1:2])
    pairs[2] = pair_step(1, 2)
    for plane in (0, 3):
        store_center(cv, plane, masked(cot, plane))
    back_done(0)
    pair_add(1, 0, pairs[0])
    pair_add(1, 2, pairs[2])
    second = all_reduce(1)
    next(second)
    back_done(1)
    for d in range(2):
        right_factor(0, bq_first, d, gate[d])
    loads[5].wait()
    wait_halo(1)
    for plane in (0, 3):
        vol[plane] = masked(vol, plane)
    pairs = []
    for a in range(3):
        grad_left(0, a, bq_first[...], vol[a : a + 2])
        pairs.append(pair_step(0, a))
        if a > 0:
            pair_add(0, a - 1, pairs[a - 1])
    error_half(0, core, True)
    pair_add(0, 2, pairs[2])
    first = all_reduce(0)
    next(first)
    for d in range(2):
        store_shifts(gv, d, gate[d])
        store_shifts(cv, 1 + d, cot[1 + d])
    wait_halo(2)
    for plane in (0, 3):
        act[plane] = jnp.maximum(masked(act, plane), jnp.zeros((CELLS, C), BF))
    grad_step(1, act, cv, 1, 0)
    grad_step(1, act, cv, 1, 1)
    next(second)
    for i in range(2, 8):
        grad_step(1, act, cv, 1, i)
    next(first)
    second_copies = next(second)
    grad_step(1, act, cv, 1, 8)
    for i in range(0, 4):
        grad_step(0, vol, gv, 0, i)
    first_copies = next(first)
    for i in range(4, 9):
        grad_step(0, vol, gv, 0, i)

    eye = (
        lax.broadcasted_iota(jnp.int32, (RANK, RANK), 0)
        == lax.broadcasted_iota(jnp.int32, (RANK, RANK), 1)
    ).astype(F32)
    rows = lax.broadcasted_iota(jnp.int32, (RANK, 2 * RANK), 0)
    tables = [None, None]

    def eliminate(l, j0, j1):
        t = tables[l]
        for j in range(j0, j1):
            row = t[j : j + 1, :] * (1.0 / t[j : j + 1, j : j + 1])
            t = jnp.where(rows == j, row, t - t[:, j : j + 1] * row)
        tables[l] = t

    right_terms(1, second_copies)
    sum_second = right_reduce(1)
    next(sum_second)
    tables[1] = gram_table(1)
    eliminate(1, 0, 4)
    right_terms(0, first_copies, lambda: eliminate(1, 4, 14))
    sum_first = right_reduce(0)
    next(sum_first)
    next(sum_second)
    tables[0] = gram_table(0)
    eliminate(1, 14, 24)
    eliminate(0, 0, 10)
    next(sum_second)
    next(sum_first)
    eliminate(1, 24, 32)
    eliminate(0, 10, 23)
    settle()
    next(sum_first)
    eliminate(0, 23, 32)
    next(sum_second)
    right = stacked_right(right_out[1])
    for k in range(27):
        part = slice(k * 256, (k + 1) * 256)
        tail[part, :] = (mat_second[part, :] - left_product(flat[1, k], right)).astype(BF)
    next(sum_first)
    settle()


def last_kernel(
    start_ref, mat_ref, left_ref, right_ref, tail_ref, err_hbm, sum_hbm, done, span, sems
):
    copies = [pltpu.make_async_copy(tail_ref, err_hbm.at[1], sems.at[0])]
    copies[0].start()
    start = start_ref[0]
    k = jnp.minimum(start // 256, 25)
    part = pl.ds(pl.multiple_of(start - k * 256, 8), ROWS // 32)
    for l in range(2):
        right = stacked_right(right_ref[l])
        for j in range(2):
            span[l, 256 * j : 256 * (j + 1), :] = left_product(left_ref[l, k + j], right) * 128.0
        copies.append(pltpu.make_async_copy(span.at[l, part], sum_hbm.at[l], sems.at[1 + l]))
        copies[-1].start()
    right = stacked_right(right_ref[0])
    for i in range(9):
        for k in range(3 * i, 3 * i + 3):
            part = slice(k * 256, (k + 1) * 256)
            done[part, :] = (mat_ref[part, :] - left_product(left_ref[0, k], right)).astype(BF)
        part = pl.ds(768 * i, 768)
        copies.append(pltpu.make_async_copy(done.at[part], err_hbm.at[0, part], sems.at[3 + i]))
        copies[-1].start()
    for copy in copies:
        copy.wait()


def per_device(volume, pre_act, cotangent, kernel_second, q_start, error):
    def rows(x):
        return x.reshape(2, CELLS, C)

    hbm = pl.BlockSpec(memory_space=pltpu.HBM)
    vmem = pl.BlockSpec(memory_space=pltpu.VMEM)
    dma = pltpu.SemaphoreType.DMA
    V = pltpu.VMEM
    mat, left, right, tail = pl.pallas_call(
        main_kernel,
        out_shape=(
            V((ROWS, C), F32), V((2, 32, 2 * RANK, C), BF), V((2, RANK, C), F32), V((ROWS, C), BF),
        ),
        in_specs=[hbm] * 5 + [vmem],
        out_specs=(vmem, vmem, vmem, vmem),
        scratch_shapes=[
            V((4, CELLS, C), BF), V((4, CELLS, C), BF), V((4, CELLS, C), BF),
            V((27, C, C), BF), V((2, ROWS, C), BF), V((3, 4, PAD, C), BF), V((3, 2, PAD, C), BF),
            V((2, PAD, 6 * RANK), BF), V((4, PAD, 6 * RANK), BF),
            V((2, 3, CELLS, C), F32), V((2, CELLS, C), BF), V((ROWS, C), F32),
            V((2, 2, 16, RANK, C), F32), V((2, 14, RANK, C), F32), V((2, 15, RANK, C), F32),
            V((2, 4, RANK, C), F32), V((2, 2, 16, RANK, C), F32),
            V((2, RANK, C), F32), V((2, 16, RANK, C), F32),
            dma((6,)), dma((3, 2)), dma((3, 2)), dma((2, 3)), dma((2, 3)), dma((2, 49)),
            dma((2, 49)), dma((2, 13)), dma((2, 13)),
        ],
        compiler_params=pltpu.CompilerParams(
            collective_id=0, has_side_effects=True, vmem_limit_bytes=MAIN_VMEM << 20
        ),
        name="main_kernel",
    )(
        rows(pre_act), rows(cotangent), rows(volume), kernel_second,
        error.reshape(2, ROWS, C), jnp.swapaxes(q_start, 1, 2),
    )
    start = (lax.axis_index("slab") * (ROWS // 32)).astype(jnp.int32).reshape(1)
    new_error, summed = pl.pallas_call(
        last_kernel,
        out_shape=(
            jax.ShapeDtypeStruct((2, ROWS, C), BF),
            jax.ShapeDtypeStruct((2, ROWS // 32, C), F32),
        ),
        in_specs=[pl.BlockSpec(memory_space=pltpu.SMEM), vmem, vmem, vmem, vmem],
        out_specs=(hbm, hbm),
        scratch_shapes=[V((ROWS, C), BF), V((2, 512, C), F32), dma((12,))],
        compiler_params=pltpu.CompilerParams(vmem_limit_bytes=LAST_VMEM << 20),
        name="last_kernel",
    )(start, mat, left, right, tail)
    return (summed, new_error.reshape(1, 1, 2, ROWS, C))


def solution(mesh):
    in_specs = (
        P("dp", "slab", None, None, None),
        P("dp", "slab", None, None, None),
        P("dp", "slab", None, None, None),
        P(),
        P(),
        P("dp", "slab", None, None, None),
    )
    out_specs = (P(None, "slab", None), P("dp", "slab", None, None, None))
    return jax.shard_map(
        per_device, mesh=mesh, in_specs=in_specs, out_specs=out_specs, check_vma=False
    )
```

```python
import functools

import jax
import jax.numpy as jnp
from jax import lax
from jax.experimental import pallas as pl
from jax.experimental.pallas import tpu as pltpu
from jax.sharding import PartitionSpec as P

BF, F32 = jnp.bfloat16, jnp.float32
MESH = pl.DeviceIdType.MESH
NT = (((1,), (1,)), ((), ()))
TN = (((0,), (0,)), ((), ()))
NN = (((1,), (0,)), ((), ()))
C, RANK, CELLS, WW, ROWS = 256, 32, 512, 32, 6912
PAD = CELLS + 2 * WW
MAIN_VMEM, LAST_VMEM = 46, 16


def mm(x, y, dims=NN):
    return lax.dot_general(x, y, dims, preferred_element_type=F32)


def split(x):
    hi = x.astype(BF)
    return hi, (x - hi.astype(F32)).astype(BF)


def precise(x, y, dims=NN):
    xh, xl = split(x)
    yh, yl = split(y)
    return mm(xh, yh, dims) + (mm(xh, yl, dims) + mm(xl, yh, dims))


def store_center(dst, plane, x):
    zero = jnp.zeros((WW, C), BF)
    dst[1, plane, 0:WW, :] = zero
    dst[1, plane, WW : WW + CELLS, :] = x
    dst[1, plane, WW + CELLS : PAD, :] = zero


def store_shifts(dst, plane, x):
    w = lax.broadcasted_iota(jnp.int32, (CELLS, C), 0) % WW
    wide = x.astype(F32)
    up = jnp.where(w == WW - 1, 0.0, pltpu.roll(wide, CELLS - 1, 0))
    down = jnp.where(w == 0, 0.0, pltpu.roll(wide, 1, 0))
    zero = jnp.zeros((WW, C), BF)
    for c, piece in enumerate((up.astype(BF), x, down.astype(BF))):
        dst[c, plane, 0:WW, :] = zero
        dst[c, plane, WW : WW + CELLS, :] = piece
        dst[c, plane, WW + CELLS : PAD, :] = zero


class Places:
    def __init__(self):
        self.y = lax.axis_index("dp")
        self.s = lax.axis_index("slab")
        self.x = self.s // 8
        self.z = (self.s // 2) % 4
        self.core = self.s % 2

    def at(self, dy, dx, dz, dcore=0):
        y = (self.y + dy) % 4
        x = (self.x + dx) % 4
        z = (self.z + dz) % 4
        core = (self.core + dcore) % 2
        return {"dp": y, "slab": x * 8 + z * 2 + core}

    def slab(self, step):
        return {"dp": self.y, "slab": (self.s + step + 32) % 32}


def left_product(both, right):
    return mm(jnp.concatenate([both[:RANK], both], 0), right, TN) * (1.0 / 128)


def stacked_right(right):
    hi, lo = split(right)
    return jnp.concatenate([lo, hi, hi], 0)


def main_kernel(
    pre_hbm, cot_hbm, vol_hbm, ker_hbm, err_hbm, qt_ref,
    mat_first, flat, right_out, tail,
    act, cot, vol, ker, err, cv, gv, bq_first, bq_second, acc, gate, mat_second, send, r0, r1, r2, fin,
    srcv, sall, local_sem, halo_send, halo_recv, pair_send, pair_recv, ar_send, ar_recv,
    s_send, s_recv,
):
    me = Places()
    s, core = me.s, me.core
    one = 1 - core

    loads = []
    for i, (src, dst) in enumerate(
        (
            (cot_hbm, cot.at[1:3]),
            (pre_hbm, act.at[1:3]),
            (err_hbm.at[1], err.at[1]),
            (ker_hbm, ker),
            (err_hbm.at[0], err.at[0]),
            (vol_hbm, vol.at[1:3]),
        )
    ):
        copy = pltpu.make_async_copy(src, dst, local_sem.at[i])
        copy.start()
        loads.append(copy)

    barrier = pltpu.get_barrier_semaphore()
    peers = [me.slab(-1), me.slab(1)]
    for i in range(1, 4):
        peers += [me.at(i, 0, 0), me.at(0, i, 0)]
        for j in range(1, 4):
            peers += [me.at(i, j, 0), me.at(i * one, i * core, j)]
    peers += [me.at(0, 0, i // 2, i % 2) for i in range(1, 8)]
    for peer in peers:
        pl.semaphore_signal(barrier, inc=1, device_id=peer, device_id_type=MESH)
    halos = []

    def send_halos():
        for i, (src, dst) in enumerate(((cot_hbm, cot), (vol_hbm, vol), (pre_hbm, act))):
            pair = []
            for j, (plane, slot, step) in enumerate(((1, 0, 1), (0, 3, -1))):
                copy = pltpu.make_async_remote_copy(
                    src_ref=src.at[plane], dst_ref=dst.at[slot],
                    send_sem=halo_send.at[i, j], recv_sem=halo_recv.at[i, j],
                    device_id=me.slab(step), device_id_type=MESH,
                )
                copy.start()
                pair.append(copy)
            halos.append(pair)

    def wait_halo(i):
        for copy in halos[i]:
            copy.wait()

    def masked(ref, plane):
        if plane == 0:
            return jnp.where(s > 0, ref[0], jnp.zeros((CELLS, C), BF))
        if plane == 3:
            return jnp.where(s < 31, ref[3], jnp.zeros((CELLS, C), BF))
        return ref[plane]

    q2 = [jnp.concatenate(split(qt_ref[l]), 0) for l in range(2)]

    def error_left(l):
        for k in range(27):
            t = mm(q2[l], err[l, k * 256 : (k + 1) * 256, :], NT)
            send[l, k % 2, k // 2] = t[:RANK] + t[RANK:]
        for k in range(27, 32):
            send[l, k % 2, k // 2] = jnp.zeros((RANK, C), F32)

    def error_half(l, hand, add):
        for t in range(14):
            k = 2 * t + hand
            row = pl.multiple_of(jnp.minimum(k, 26) * 256, 256)
            value = mm(q2[l], err[l, pl.ds(row, 256), :], NT)
            value = jnp.where(k < 27, value[:RANK] + value[RANK:], 0.0)
            send[l, hand, t] = send[l, hand, t] + value if add else value

    def right_factor(l, dst, d, x):
        t = mm(x, q2[l], NT)
        t = t[:, :RANK] + t[:, RANK:]
        w = lax.broadcasted_iota(jnp.int32, (CELLS, RANK), 0) % WW
        up = jnp.where(w == WW - 1, 0.0, pltpu.roll(t, CELLS - 1, 0))
        down = jnp.where(w == 0, 0.0, pltpu.roll(t, 1, 0))
        zero = jnp.zeros((WW, 6 * RANK), BF)
        dst[d, 0:WW, :] = zero
        dst[d, WW : WW + CELLS, :] = jnp.concatenate([*split(up), *split(t), *split(down)], 1)
        dst[d, WW + CELLS : PAD, :] = zero

    def grad_left(l, a, factor, planes):
        size = planes.shape[0] * CELLS
        for b in range(3):
            r = (2 - b) * WW
            x = factor[:, r : r + CELLS, :].reshape(size, 6 * RANK)
            t = mm(x, planes[...].reshape(size, C), TN)
            for c in range(3):
                k = 9 * a + 3 * b + c
                piece = t[64 * c : 64 * c + 32] + t[64 * c + 32 : 64 * c + 64]
                send[l, k % 2, k // 2] = send[l, k % 2, k // 2] + piece

    near = [(min(i, 4 - i) + min(j, 4 - j), i, j) for i in range(4) for j in range(4)]
    others = [(i, j) for d, i, j in sorted(near, reverse=True) if d > 0]

    def plane_index(l, hand, i, j):
        if l == 1:
            return (me.y + i) % 4 * 4 + (me.x + j) % 4
        return (me.y * (1 - hand) + me.x * hand + i) % 4 * 4 + (me.z + j) % 4

    def plane_peer(l, i, j):
        return me.at(i, j, 0) if l == 1 else me.at(i * one, i * core, j)

    def axis_index(l):
        return me.z if l == 1 else me.x * one + me.y * core

    def axis_peer(l, i):
        return me.at(0, 0, i) if l == 1 else me.at(i * core, i * one, 0)

    pending, forwards = [], {}

    def push(src, dst, sems, l, n, peer):
        copy = pltpu.make_async_remote_copy(
            src_ref=src, dst_ref=dst, send_sem=sems[0].at[l, n], recv_sem=sems[1].at[l, n],
            device_id=peer, device_id_type=MESH,
        )
        copy.start()
        pending.append(copy)
        return copy

    ar_sems = (ar_send, ar_recv)
    pair_sems = (pair_send, pair_recv)
    bounds = (((0, 4), (4, 9), (9, 14)), ((0, 5), (5, 9), (9, 14)))

    def settle():
        for copy in pending:
            copy.wait_send()
        pending.clear()

    def pair_step(l, n):
        low, high = bounds[l][n]
        part = pl.ds(low, high - low)
        return push(
            send.at[l, one, part], r0.at[l, part], pair_sems, l, n, me.at(0, 0, 0, 1)
        )

    def pair_add(l, n, copy):
        copy.wait_recv()
        for t in range(*bounds[l][n]):
            send[l, core, t] = send[l, core, t] + r0[l, t]

    def all_reduce(l):
        here = plane_index(l, core, 0, 0)
        copies = [
            push(
                send.at[l, core, plane_index(l, core, i, j)], r1.at[l, n],
                ar_sems, l, n, plane_peer(l, i, j),
            )
            for n, (i, j) in enumerate(others)
        ]
        yield
        total = send[l, core, here]
        for n in range(14, -1, -1):
            copies[n].wait_recv()
            total = total + r1[l, n]
        i3 = axis_index(l)
        r2[l, i3] = total
        copies = [
            push(r2.at[l, i3], r2.at[l, i3], ar_sems, l, 14 + i, axis_peer(l, i))
            for i in range(1, 4)
        ]
        yield
        for copy in copies:
            copy.wait_recv()
        fin[l, core, here] = (r2[l, 0] + r2[l, 1]) + (r2[l, 2] + r2[l, 3])
        copies = [
            push(
                fin.at[l, core, here], fin.at[l, core, here], ar_sems, l, 18 + n,
                plane_peer(l, i, j),
            )
            for n, (i, j) in enumerate(others)
        ]
        forward(l, 0, 0, 0)
        yield copies

    def forward(l, n, i, j):
        slot = fin.at[l, core, plane_index(l, core, i, j)]
        forwards[l, n] = push(slot, slot, ar_sems, l, 33 + n, me.at(0, 0, 0, 1))

    def right_tap(l, hand, tap, sums):
        mat = mat_first if l == 0 else mat_second
        k = 2 * tap + hand
        row = pl.multiple_of(jnp.minimum(k, 26) * 256, 256)
        mh, ml = split(mat[pl.ds(row, 256), :])
        both = jnp.concatenate(split(fin[l, hand, tap]), 0)
        flat[l, k] = both
        t = mm(both, mh)
        return sums + (t[:RANK] + (t[RANK:] + mm(both[:RANK], ml)))

    def gram_table(l):
        gram = jnp.zeros((2 * RANK, 2 * RANK), F32)
        for k in range(27):
            gram = gram + mm(flat[l, k], flat[l, k], NT)
        gram = (gram[:RANK, :RANK] + gram[RANK:, RANK:]) + (
            gram[:RANK, RANK:] + gram[RANK:, :RANK]
        )
        return jnp.concatenate([gram, eye], 1)

    def right_terms(l, copies, middle=lambda: None):
        sums = jnp.zeros((RANK, C), F32)
        done = [(0, 0)]
        for low, high in ((7, 15), (0, 7)):
            for n in range(high - 1, low - 1, -1):
                sender = others[n]
                source = (-sender[0]) % 4, (-sender[1]) % 4
                copies[n].wait_recv()
                forward(l, 1 + n, *source)
                done.append(source)
            for i, j in done:
                sums = right_tap(l, core, plane_index(l, core, i, j), sums)
            done = []
        for n in [0] + list(range(15, 0, -1)):
            forwards[l, n].wait_recv()
        middle()
        for t in range(14):
            sums = right_tap(l, one, t, sums)
        srcv[l] = sums

    def right_reduce(l):
        s_sems = (s_send, s_recv)
        mine = srcv[l]
        for n, (index, step) in enumerate(((me.y, (1, 0, 0)), (me.x, (0, 1, 0)))):
            slot = 4 * n + index
            sall[l, slot] = mine
            copies = [
                push(
                    sall.at[l, slot], sall.at[l, slot], s_sems, l, 3 * n + i - 1,
                    me.at(*(i * v for v in step)),
                )
                for i in range(1, 4)
            ]
            yield
            for copy in copies:
                copy.wait_recv()
            mine = (sall[l, 4 * n] + sall[l, 4 * n + 1]) + (sall[l, 4 * n + 2] + sall[l, 4 * n + 3])
        slot = 8 + 2 * me.z + core
        sall[l, slot] = mine
        copies = [
            push(sall.at[l, slot], sall.at[l, slot], s_sems, l, 5 + i, me.at(0, 0, i // 2, i % 2))
            for i in range(1, 8)
        ]
        yield
        for copy in copies:
            copy.wait_recv()
        total = [sall[l, 8 + 2 * i] + sall[l, 9 + 2 * i] for i in range(4)]
        right_out[l] = precise(tables[l][:, RANK:], (total[0] + total[1]) + (total[2] + total[3]))
        yield

    def grad_step(l, planes, source, first, i):
        b, c = i // 3, i % 3
        r = (2 - b) * WW
        right = source[c, first : first + 2, r : r + CELLS, :].reshape(2 * CELLS, C)
        for a in range(3):
            rows = slice((9 * a + i) * 256, (9 * a + i + 1) * 256)
            g = mm(planes[a : a + 2].reshape(2 * CELLS, C), right, TN)
            mat = mat_first if l == 0 else mat_second
            mat[rows, :] = g + err[l, rows, :].astype(F32)

    def back_part(d, a, c):
        x = jnp.concatenate(
            [cv[1, d + 2 - a, (2 - b) * WW : (2 - b) * WW + CELLS, :] for b in range(3)], 1
        )
        return mm(x, jnp.concatenate([ker[9 * a + 3 * b + c] for b in range(3)], 1), NT)

    def back_done(d):
        parts = [acc[d, c] + back_part(d, 2 - 2 * d, c) for c in range(3)]
        w = lax.broadcasted_iota(jnp.int32, (CELLS, C), 0) % WW
        up = jnp.where(w == WW - 1, 0.0, pltpu.roll(parts[0], CELLS - 1, 0))
        down = jnp.where(w == 0, 0.0, pltpu.roll(parts[2], 1, 0))
        total = parts[1] + up + down
        gate[d] = jnp.where(act[1 + d] > 0, total, 0.0).astype(BF)

    loads[0].wait()
    for plane in (1, 2):
        right_factor(1, bq_second, plane, cot[plane])
    loads[1].wait()
    for plane in (1, 2):
        act[plane] = jnp.maximum(act[plane], jnp.zeros((CELLS, C), BF))
    loads[2].wait()
    error_left(1)
    grad_left(1, 1, bq_second[1:3], act[1:3])
    pl.semaphore_wait(barrier, len(peers))
    send_halos()
    pairs = {1: pair_step(1, 1)}
    grad_left(1, 0, bq_second[2:3], act[1:2])
    grad_left(1, 2, bq_second[1:2], act[2:3])
    for plane in (1, 2):
        store_center(cv, plane, cot[plane])
    loads[3].wait()
    for c in range(3):
        acc[0, c] = back_part(0, 0, c) + back_part(0, 1, c)
        acc[1, c] = back_part(1, 1, c) + back_part(1, 2, c)
    pair_add(1, 1, pairs[1])
    loads[4].wait()
    error_half(0, one, False)
    for t in range(16):
        send[0, core, t] = jnp.zeros((RANK, C), F32)
    wait_halo(0)
    for plane in (0, 3):
        right_factor(1, bq_second, plane, masked(cot, plane))
    grad_left(1, 0, bq_second[3:4], act[2:3])
    pairs[0] = pair_step(1, 0)
    grad_left(1, 2, bq_second[0:1], act[1:2])
    pairs[2] = pair_step(1, 2)
    for plane in (0, 3):
        store_center(cv, plane, masked(cot, plane))
    back_done(0)
    pair_add(1, 0, pairs[0])
    pair_add(1, 2, pairs[2])
    second = all_reduce(1)
    next(second)
    back_done(1)
    for d in range(2):
        right_factor(0, bq_first, d, gate[d])
    loads[5].wait()
    wait_halo(1)
    for plane in (0, 3):
        vol[plane] = masked(vol, plane)
    pairs = []
    for a in range(3):
        grad_left(0, a, bq_first[...], vol[a : a + 2])
        pairs.append(pair_step(0, a))
        if a > 0:
            pair_add(0, a - 1, pairs[a - 1])
    error_half(0, core, True)
    pair_add(0, 2, pairs[2])
    first = all_reduce(0)
    next(first)
    for d in range(2):
        store_shifts(gv, d, gate[d])
        store_shifts(cv, 1 + d, cot[1 + d])
    wait_halo(2)
    for plane in (0, 3):
        act[plane] = jnp.maximum(masked(act, plane), jnp.zeros((CELLS, C), BF))
    grad_step(1, act, cv, 1, 0)
    grad_step(1, act, cv, 1, 1)
    next(second)
    for i in range(2, 8):
        grad_step(1, act, cv, 1, i)
    next(first)
    second_copies = next(second)
    grad_step(1, act, cv, 1, 8)
    for i in range(0, 4):
        grad_step(0, vol, gv, 0, i)
    first_copies = next(first)
    for i in range(4, 9):
        grad_step(0, vol, gv, 0, i)

    eye = (
        lax.broadcasted_iota(jnp.int32, (RANK, RANK), 0)
        == lax.broadcasted_iota(jnp.int32, (RANK, RANK), 1)
    ).astype(F32)
    rows = lax.broadcasted_iota(jnp.int32, (RANK, 2 * RANK), 0)
    tables = [None, None]

    def eliminate(l, j0, j1):
        t = tables[l]
        for j in range(j0, j1):
            row = t[j : j + 1, :] * (1.0 / t[j : j + 1, j : j + 1])
            t = jnp.where(rows == j, row, t - t[:, j : j + 1] * row)
        tables[l] = t

    right_terms(1, second_copies)
    sum_second = right_reduce(1)
    next(sum_second)
    tables[1] = gram_table(1)
    eliminate(1, 0, 4)
    right_terms(0, first_copies, lambda: eliminate(1, 4, 14))
    sum_first = right_reduce(0)
    next(sum_first)
    next(sum_second)
    tables[0] = gram_table(0)
    eliminate(1, 14, 24)
    eliminate(0, 0, 10)
    next(sum_second)
    next(sum_first)
    eliminate(1, 24, 32)
    eliminate(0, 10, 23)
    settle()
    next(sum_first)
    eliminate(0, 23, 32)
    next(sum_second)
    right = stacked_right(right_out[1])
    for k in range(27):
        part = slice(k * 256, (k + 1) * 256)
        tail[part, :] = (mat_second[part, :] - left_product(flat[1, k], right)).astype(BF)
    next(sum_first)
    settle()


def last_kernel(
    start_ref, mat_ref, left_ref, right_ref, tail_ref, err_hbm, sum_hbm, done, span, sems
):
    copies = [pltpu.make_async_copy(tail_ref, err_hbm.at[1], sems.at[0])]
    copies[0].start()
    start = start_ref[0]
    k = jnp.minimum(start // 256, 25)
    part = pl.ds(pl.multiple_of(start - k * 256, 8), ROWS // 32)
    for l in range(2):
        right = stacked_right(right_ref[l])
        for j in range(2):
            span[l, 256 * j : 256 * (j + 1), :] = left_product(left_ref[l, k + j], right) * 128.0
        copies.append(pltpu.make_async_copy(span.at[l, part], sum_hbm.at[l], sems.at[1 + l]))
        copies[-1].start()
    right = stacked_right(right_ref[0])
    for i in range(9):
        both = jnp.concatenate([left_ref[0, k] for k in range(3 * i, 3 * i + 3)], 1)
        part = slice(768 * i, 768 * (i + 1))
        done[part, :] = (mat_ref[part, :] - left_product(both, right)).astype(BF)
        part = pl.ds(768 * i, 768)
        copies.append(pltpu.make_async_copy(done.at[part], err_hbm.at[0, part], sems.at[3 + i]))
        copies[-1].start()
    for copy in copies:
        copy.wait()


def per_device(volume, pre_act, cotangent, kernel_second, q_start, error):
    def rows(x):
        return x.reshape(2, CELLS, C)

    hbm = pl.BlockSpec(memory_space=pltpu.HBM)
    vmem = pl.BlockSpec(memory_space=pltpu.VMEM)
    dma = pltpu.SemaphoreType.DMA
    V = pltpu.VMEM
    mat, left, right, tail = pl.pallas_call(
        main_kernel,
        out_shape=(
            V((ROWS, C), F32), V((2, 32, 2 * RANK, C), BF), V((2, RANK, C), F32), V((ROWS, C), BF),
        ),
        in_specs=[hbm] * 5 + [vmem],
        out_specs=(vmem, vmem, vmem, vmem),
        scratch_shapes=[
            V((4, CELLS, C), BF), V((4, CELLS, C), BF), V((4, CELLS, C), BF),
            V((27, C, C), BF), V((2, ROWS, C), BF), V((3, 4, PAD, C), BF), V((3, 2, PAD, C), BF),
            V((2, PAD, 6 * RANK), BF), V((4, PAD, 6 * RANK), BF),
            V((2, 3, CELLS, C), F32), V((2, CELLS, C), BF), V((ROWS, C), F32),
            V((2, 2, 16, RANK, C), F32), V((2, 14, RANK, C), F32), V((2, 15, RANK, C), F32),
            V((2, 4, RANK, C), F32), V((2, 2, 16, RANK, C), F32),
            V((2, RANK, C), F32), V((2, 16, RANK, C), F32),
            dma((6,)), dma((3, 2)), dma((3, 2)), dma((2, 3)), dma((2, 3)), dma((2, 49)),
            dma((2, 49)), dma((2, 13)), dma((2, 13)),
        ],
        compiler_params=pltpu.CompilerParams(
            collective_id=0, has_side_effects=True, vmem_limit_bytes=MAIN_VMEM << 20
        ),
        name="main_kernel",
    )(
        rows(pre_act), rows(cotangent), rows(volume), kernel_second,
        error.reshape(2, ROWS, C), jnp.swapaxes(q_start, 1, 2),
    )
    start = (lax.axis_index("slab") * (ROWS // 32)).astype(jnp.int32).reshape(1)
    new_error, summed = pl.pallas_call(
        last_kernel,
        out_shape=(
            jax.ShapeDtypeStruct((2, ROWS, C), BF),
            jax.ShapeDtypeStruct((2, ROWS // 32, C), F32),
        ),
        in_specs=[pl.BlockSpec(memory_space=pltpu.SMEM), vmem, vmem, vmem, vmem],
        out_specs=(hbm, hbm),
        scratch_shapes=[V((ROWS, C), BF), V((2, 512, C), F32), dma((12,))],
        compiler_params=pltpu.CompilerParams(vmem_limit_bytes=LAST_VMEM << 20),
        name="last_kernel",
    )(start, mat, left, right, tail)
    return (summed, new_error.reshape(1, 1, 2, ROWS, C))


def solution(mesh):
    in_specs = (
        P("dp", "slab", None, None, None),
        P("dp", "slab", None, None, None),
        P("dp", "slab", None, None, None),
        P(),
        P(),
        P("dp", "slab", None, None, None),
    )
    out_specs = (P(None, "slab", None), P("dp", "slab", None, None, None))
    return jax.shard_map(
        per_device, mesh=mesh, in_specs=in_specs, out_specs=out_specs, check_vma=False
    )
```
